128 devices in a mesh: row: 8 (over z, y_hi), col: 16 (over x, y_lo, core).
Axes of the slice: x: 4, y: 4 (y_hi: 2, y_lo: 2; y = y_hi * 2 + y_lo), z: 4, core: 2. Of those that a mesh axis runs over, the one named last changes fastest.
Arguments:
- pair: bfloat16 [768, 768, 128], P('row', 'col'), may hold values from -6 to 6
- residue_mask: int32 [768], replicated, may hold values 0 or 1
- out_ab_weight: bfloat16 [128, 512], replicated, may hold values from -0.5 to 0.5
- out_gate_weight: bfloat16 [128, 128], replicated, may hold values from -0.5 to 0.5
- out_z_weight: bfloat16 [128, 128], replicated, may hold values from -0.5 to 0.5
- in_ab_weight: bfloat16 [128, 512], replicated, may hold values from -0.5 to 0.5
- in_gate_weight: bfloat16 [128, 128], replicated, may hold values from -0.5 to 0.5
- in_z_weight: bfloat16 [128, 128], replicated, may hold values from -0.5 to 0.5
- trans_up: bfloat16 [128, 512], replicated, may hold values from -0.5 to 0.5
- trans_down: bfloat16 [512, 128], replicated, may hold values from -0.25 to 0.25
Outputs:
- updated_pair: bfloat16 [768, 768, 128], P('row', 'col')
The draws below stay inside these ranges and needn't reach their ends.
All inputs are finite; a program needn't handle non-finite values.
Results may differ from the reference program's by a relative error of at most 0.02.
Values may be sent and summed in bfloat16 or wider, within the bound.
A program may use at most 256 MiB of HBM per device.

```python
import jax
import jax.numpy as jnp
from jax import lax

PAIR = 128
HIDDEN_SIZE = 128
EXPAND = 512
TJ = 48
RES = 768
TI = 96
N_ROW = 8
N_COL = 16


def set_ends(entries, rng, least, high):
    index_at = [jax.random.randint(jax.random.fold_in(rng, axis), (), 0, length) for axis, length in enumerate(entries.shape)]
    main_axis = entries.shape.index(max(entries.shape))
    neighbour = index_at[:main_axis] + [(index_at[main_axis] + 1) % entries.shape[main_axis]] + index_at[main_axis + 1:]
    return entries.at[tuple(index_at)].set(least).at[tuple(neighbour)].set(high)


def levels(stream_key, shape, pieces, least, largest):
    def one(axis_at, parts):
        heights = jax.random.uniform(jax.random.fold_in(jax.random.fold_in(stream_key, 6), axis_at), (parts,), jnp.float32, least / len(pieces), largest / len(pieces))
        return jnp.repeat(jnp.exp(heights), shape[axis_at] // parts).reshape((-1,) + (1,) * (len(shape) - axis_at - 1))

    level = one(*pieces[0])
    for cut in pieces[1:]:
        level = level * one(*cut)
    return level


def bell_draw(stream_key, extent, deviation, reach, shards=(), held_as=jnp.bfloat16):
    drawn = jax.random.normal(stream_key, extent, jnp.float32) * deviation
    if len(shards) > 0:
        drawn = levels(stream_key, extent, shards, -0.22, 0.18) * drawn
    return jnp.clip(drawn, min=-reach, max=reach).astype(held_as)


def setup_inputs(seed: int = 0) -> dict:
    key_of = jax.random.split(jax.random.key(seed), 11)
    pair = bell_draw(key_of[0], (RES, RES, PAIR), 1.0, 6.0, ((0, 8), (1, 16)))
    residue_mask = set_ends((jax.random.randint(key_of[1], (RES,), 0, 8) < 7).astype(jnp.int32), jax.random.fold_in(key_of[1], 1), 0, 1)
    out_ab_weight = bell_draw(key_of[2], (PAIR, 4 * HIDDEN_SIZE), PAIR ** -0.5, 0.5)
    out_gate_weight = bell_draw(key_of[3], (PAIR, PAIR), PAIR ** -0.5, 0.5)
    out_z_weight = bell_draw(key_of[4], (HIDDEN_SIZE, PAIR), HIDDEN_SIZE ** -0.5, 0.5)
    in_ab_weight = bell_draw(key_of[5], (PAIR, 4 * HIDDEN_SIZE), PAIR ** -0.5, 0.5)
    in_gate_weight = bell_draw(key_of[6], (PAIR, PAIR), PAIR ** -0.5, 0.5)
    in_z_weight = bell_draw(key_of[7], (HIDDEN_SIZE, PAIR), HIDDEN_SIZE ** -0.5, 0.5)
    trans_up = bell_draw(key_of[8], (PAIR, EXPAND), PAIR ** -0.5, 0.5)
    trans_down = bell_draw(key_of[9], (EXPAND, PAIR), EXPAND ** -0.5, 0.25)
    return dict(pair=pair, residue_mask=residue_mask, out_ab_weight=out_ab_weight, out_gate_weight=out_gate_weight, out_z_weight=out_z_weight, in_ab_weight=in_ab_weight, in_gate_weight=in_gate_weight, in_z_weight=in_z_weight, trans_up=trans_up, trans_down=trans_down)


EPS = 1e-05

def layer_norm(values):
    values = values.astype(jnp.float32)
    center = values - lax.optimization_barrier(jnp.mean(values, axis=-1, keepdims=True))
    return center * lax.rsqrt(lax.optimization_barrier(jnp.mean(center * center, axis=-1, keepdims=True)) + EPS)

def project_matrix(normed, weight):
    return jnp.einsum('ijc,cd->ijd', normed.astype(jnp.float32), weight.astype(jnp.float32))

def operands(normed, weight, pair_mask):
    projected = project_matrix(normed, weight)
    hidden = HIDDEN_SIZE
    left = pair_mask[:, :, None] * jax.nn.sigmoid(projected[:, :, hidden:2 * hidden]) * projected[:, :, :hidden]
    right = pair_mask[:, :, None] * jax.nn.sigmoid(projected[:, :, 3 * hidden:]) * projected[:, :, 2 * hidden:3 * hidden]
    return (left.astype(jnp.bfloat16), right.astype(jnp.bfloat16))

def block_sum(left_blocks, right_blocks, form):

    def step(total, blocks):
        left_part, right_part = blocks
        part = jnp.einsum(form, left_part.astype(jnp.float32), right_part.astype(jnp.float32))
        rounded = lax.optimization_barrier(part.astype(jnp.bfloat16)).astype(jnp.float32)
        return (total + rounded, None)
    start = jnp.zeros((RES, RES, HIDDEN_SIZE), jnp.float32)
    total, unused = lax.scan(step, start, (left_blocks, right_blocks))
    return total

def finish(triangle, gating, z_weight, current):
    normed = layer_norm(triangle).astype(jnp.bfloat16)
    update = gating * project_matrix(normed, z_weight)
    return (current.astype(jnp.float32) + update).astype(jnp.bfloat16)

def reference(pair, residue_mask, out_ab_weight, out_gate_weight, out_z_weight, in_ab_weight, in_gate_weight, in_z_weight, trans_up, trans_down):
    present = residue_mask.astype(jnp.float32)
    pair_mask = present[:, None] * present[None, :]
    normed = layer_norm(pair).astype(jnp.bfloat16)
    left, right = operands(normed, out_ab_weight, pair_mask)
    gating = jax.nn.sigmoid(project_matrix(normed, out_gate_weight))
    left_blocks = jnp.transpose(left.reshape(RES, N_COL, TJ, HIDDEN_SIZE), (1, 0, 2, 3))
    right_blocks = jnp.transpose(right.reshape(RES, N_COL, TJ, HIDDEN_SIZE), (1, 0, 2, 3))
    triangle = block_sum(left_blocks, right_blocks, 'ikh,jkh->ijh')
    updated = finish(triangle, gating, out_z_weight, pair)
    normed_in = layer_norm(updated).astype(jnp.bfloat16)
    left_in, right_in = operands(normed_in, in_ab_weight, pair_mask)
    gating_in = jax.nn.sigmoid(project_matrix(normed_in, in_gate_weight))
    triangle_in = block_sum(left_in.reshape(N_ROW, TI, RES, HIDDEN_SIZE), right_in.reshape(N_ROW, TI, RES, HIDDEN_SIZE), 'kih,kjh->ijh')
    second = finish(triangle_in, gating_in, in_z_weight, updated)
    normed_out = layer_norm(second).astype(jnp.bfloat16)
    expanded = jax.nn.relu(project_matrix(normed_out, trans_up)).astype(jnp.bfloat16)
    return (second.astype(jnp.float32) + project_matrix(expanded, trans_down)).astype(jnp.bfloat16)
```

```python
import jax
import jax.numpy as jnp
from jax import lax
from jax.sharding import PartitionSpec as P

EPS = 1e-05
AXES = ("row", "col")


def layer_norm(values, axis):
    values = values.astype(jnp.float32)
    center = values - jnp.mean(values, axis=axis, keepdims=True)
    return center * lax.rsqrt(jnp.mean(center * center, axis=axis, keepdims=True) + EPS)


def project(weight, normed):
    return lax.dot_general(
        weight, normed, (((0,), (0,)), ((), ())), preferred_element_type=jnp.float32
    )


def operands(normed, weight, mask):
    hidden = weight.shape[1] // 4
    p = project(weight, normed)
    left = mask * jax.nn.sigmoid(p[hidden : 2 * hidden]) * p[:hidden]
    right = mask * jax.nn.sigmoid(p[3 * hidden :]) * p[2 * hidden : 3 * hidden]
    return left.astype(jnp.bfloat16), right.astype(jnp.bfloat16)


def finish(triangle, gating, z_weight, current):
    normed = layer_norm(triangle, 0).astype(jnp.bfloat16)
    return (current.astype(jnp.float32) + gating * project(z_weight, normed)).astype(jnp.bfloat16)


def triangle(left, right, rows, cols, n_row, n_col, form):
    hidden = left.shape[0]
    both = jnp.stack([left, right], axis=1)
    moved = lax.all_to_all(both, AXES, 0, 0, tiled=True)
    whole = moved.reshape(n_row, n_col, 2, rows, cols).transpose(2, 0, 3, 1, 4)
    whole = whole.reshape(2, n_row * rows, n_col * cols)
    sums = jnp.einsum(form, whole[0], whole[1], preferred_element_type=jnp.float32)
    sums = sums.astype(jnp.bfloat16).reshape(n_row, rows, n_col, cols).transpose(0, 2, 1, 3)
    back = lax.all_to_all(sums.reshape(hidden, rows * cols), AXES, 0, 0, tiled=True)
    return back


def body(
    pair,
    residue_mask,
    out_ab_weight,
    out_gate_weight,
    out_z_weight,
    in_ab_weight,
    in_gate_weight,
    in_z_weight,
    trans_up,
    trans_down,
):
    n_row, n_col = lax.axis_size("row"), lax.axis_size("col")
    rows, cols, channels = pair.shape
    present = residue_mask.astype(jnp.float32)
    mask_rows = lax.dynamic_slice_in_dim(present, lax.axis_index("row") * rows, rows)
    mask_cols = lax.dynamic_slice_in_dim(present, lax.axis_index("col") * cols, cols)
    mask = (mask_rows[:, None] * mask_cols[None, :]).reshape(1, rows * cols)
    current = pair.reshape(rows * cols, channels).T
    for ab, gate, z, form in (
        (out_ab_weight, out_gate_weight, out_z_weight, "ik,jk->ij"),
        (in_ab_weight, in_gate_weight, in_z_weight, "ki,kj->ij"),
    ):
        normed = layer_norm(current, 0).astype(jnp.bfloat16)
        left, right = operands(normed, ab, mask)
        gating = jax.nn.sigmoid(project(gate, normed))
        sums = triangle(left, right, rows, cols, n_row, n_col, form)
        current = finish(sums, gating, z, current)
    normed = layer_norm(current, 0).astype(jnp.bfloat16)
    expanded = jax.nn.relu(project(trans_up, normed)).astype(jnp.bfloat16)
    out = (current.astype(jnp.float32) + project(trans_down, expanded)).astype(jnp.bfloat16)
    return out.T.reshape(rows, cols, channels)


def solution(mesh):
    placed = (P("row", "col", None), P(), P(), P(), P(), P(), P(), P(), P(), P())
    return jax.shard_map(
        body, mesh=mesh, in_specs=placed, out_specs=P("row", "col", None), check_vma=False
    )
```

```python
import functools

import jax
import jax.numpy as jnp
from jax import lax
from jax.experimental import pallas as pl
from jax.experimental.pallas import tpu as pltpu
from jax.sharding import PartitionSpec as P

EPS = 1e-05
AXES = ("row", "col")
LANES = 128
SUB = 8
RUN = 16
GROUP = 4
BF16 = jnp.bfloat16
F32 = jnp.float32


def norm(x):
    center = x - jnp.mean(x, axis=0, keepdims=True)
    return center * lax.rsqrt(jnp.mean(center * center, axis=0, keepdims=True) + EPS)


def sigmoid(x):
    return 0.5 * jnp.tanh(0.5 * x) + 0.5


def dot(a, b):
    return jnp.dot(a, b, preferred_element_type=F32)


def turned(w_ref):
    return w_ref[...].astype(F32).T.astype(BF16)


def emit_operands(current, ab, gate, mask, chunk, chunks, flat, gating_ref):
    normed = norm(current).astype(BF16)
    hidden = ab.shape[0] // 4
    width = current.shape[1]
    p = dot(ab, normed)
    left = mask * sigmoid(p[hidden : 2 * hidden]) * p[:hidden]
    right = mask * sigmoid(p[3 * hidden :]) * p[2 * hidden : 3 * hidden]
    for j in range(width // LANES):
        lanes = slice(j * LANES, (j + 1) * LANES)
        flat[pl.ds(chunk + j, hidden, stride=2 * chunks), :] = left[:, lanes]
        flat[pl.ds(chunks + chunk + j, hidden, stride=2 * chunks), :] = right[:, lanes]
    here = pl.ds(pl.multiple_of(chunk * LANES, LANES), width)
    gating_ref[:, here] = sigmoid(dot(gate, normed))


def pack(flat, out_ref):
    n, rows = out_ref.shape[0], out_ref.shape[1]

    def step(i, _):
        out_ref[i] = flat[pl.ds(pl.multiple_of(i * rows, 4), rows), :].astype(out_ref.dtype)
        return 0

    lax.fori_loop(0, n, step, 0, unroll=4)


def unpack(in_ref, flat):
    n, rows = in_ref.shape[0], in_ref.shape[1]

    def step(i, _):
        flat[pl.ds(pl.multiple_of(i * rows, 4), rows), :] = in_ref[i].astype(F32)
        return 0

    lax.fori_loop(0, n, step, 0, unroll=4)


def group_mask(mask_ref, chunk):
    rows = [mask_ref[pl.ds(chunk + j, 1), :] for j in range(GROUP)]
    return jnp.concatenate(rows, axis=1)


def first_kernel(x_ref, mask_ref, ab_ref, gate_ref, out_ref, gating_ref, current_ref, flat):
    rows, cols, channels = x_ref.shape
    n_a, n_b = rows // SUB, cols // RUN
    chunks = n_a * n_b
    ab, gate = turned(ab_ref), turned(gate_ref)
    per = n_a // GROUP

    def step(g, _):
        b = g // per
        a = g % per
        block = x_ref[
            pl.ds(pl.multiple_of(a * GROUP * SUB, SUB), GROUP * SUB),
            pl.ds(pl.multiple_of(b * RUN, RUN), RUN),
            :,
        ]
        current = block.astype(F32).reshape(GROUP * LANES, channels).T
        here = pl.ds(pl.multiple_of(g * GROUP * LANES, LANES), GROUP * LANES)
        current_ref[:, here] = current.astype(BF16)
        chunk = g * GROUP
        emit_operands(
            current, ab, gate, group_mask(mask_ref, chunk), chunk, chunks, flat, gating_ref
        )
        return 0

    lax.fori_loop(0, chunks // GROUP, step, 0)
    pack(flat, out_ref)


def finish(flat_in, chunk, chunks, z, gating, current):
    channels = current.shape[0]
    triangle = jnp.concatenate(
        [flat_in[pl.ds(chunk + j, channels, stride=chunks), :] for j in range(GROUP)], axis=1
    )
    update = gating * dot(z, norm(triangle).astype(BF16))
    return (current.astype(F32) + update).astype(BF16)


def middle_kernel(
    t_ref, current_in, gating_in, mask_ref, z_ref, ab_ref, gate_ref,
    out_ref, gating_ref, current_ref, flat_in, flat,
):
    chunks = t_ref.shape[1]
    z, ab, gate = turned(z_ref), turned(ab_ref), turned(gate_ref)
    unpack(t_ref, flat_in)

    def step(g, _):
        chunk = g * GROUP
        here = pl.ds(pl.multiple_of(chunk * LANES, LANES), GROUP * LANES)
        current = finish(flat_in, chunk, chunks, z, gating_in[:, here], current_in[:, here])
        current_ref[:, here] = current
        emit_operands(
            current.astype(F32), ab, gate, group_mask(mask_ref, chunk), chunk, chunks, flat,
            gating_ref,
        )
        return 0

    lax.fori_loop(0, chunks // GROUP, step, 0)
    pack(flat, out_ref)


def last_kernel(
    t_ref, current_in, gating_in, z_ref, up_ref, down_ref, out_ref, flat_in
):
    chunks = t_ref.shape[1]
    rows, cols, channels = out_ref.shape
    per = (rows // SUB) // GROUP
    z, up, down = turned(z_ref), turned(up_ref), turned(down_ref)
    unpack(t_ref, flat_in)

    def step(g, _):
        chunk = g * GROUP
        here = pl.ds(pl.multiple_of(chunk * LANES, LANES), GROUP * LANES)
        current = finish(flat_in, chunk, chunks, z, gating_in[:, here], current_in[:, here])
        current = current.astype(F32)
        expanded = jnp.maximum(dot(up, norm(current).astype(BF16)), 0.0).astype(BF16)
        result = current + dot(down, expanded)
        b = g // per
        a = g % per
        out_ref[
            pl.ds(pl.multiple_of(a * GROUP * SUB, SUB), GROUP * SUB),
            pl.ds(pl.multiple_of(b * RUN, RUN), RUN),
            :,
        ] = result.T.reshape(GROUP * SUB, RUN, channels).astype(out_ref.dtype)
        return 0

    lax.fori_loop(0, chunks // GROUP, step, 0)


def exchange(parts):
    group = lax.broadcasted_iota(jnp.int32, parts[0].shape, 1) // RUN
    parts = list(parts)
    for bit in (1, 2, 4):
        chosen = (group // bit) % 2 == 1
        for i in range(8):
            if i & bit:
                continue
            low, high = parts[i], parts[i + bit]
            parts[i] = jnp.where(chosen, pltpu.roll(high, RUN * bit, 1), low)
            parts[i + bit] = jnp.where(chosen, high, pltpu.roll(low, LANES - RUN * bit, 1))
    return parts


def triangle_kernel(n_row, n_col, n_a, n_b, outgoing, in_ref, out_ref, flat, mats, sums, flat_out):
    chunks = n_a * n_b
    size = n_row * n_a * SUB
    tile = n_row * n_a
    unpack(in_ref, flat)

    def place(a, parity, b, a_lo):
        t = a // (n_a // 2)
        rest = a % (n_a // 2)
        return t * (n_b * LANES) + (rest // 2) * LANES + (rest % 2) * SUB + a_lo

    for operand in range(2):
        scatter = outgoing and operand == 1
        for parity in range(2):
            for b in range(n_b):
                column = (parity * n_b + b) * LANES

                def step(i, _, operand=operand, scatter=scatter, parity=parity, b=b, column=column):
                    halves = []
                    for half in range(2):
                        a = i * 2 + half
                        parts = [
                            flat[
                                pl.ds(
                                    (2 * c + parity) * 2 * chunks + operand * chunks + b * n_a + a,
                                    n_row,
                                    stride=n_col * 2 * chunks,
                                ),
                                :,
                            ]
                            for c in range(8)
                        ]
                        halves.append(exchange(parts))
                    for a_lo in range(8):
                        if scatter:
                            for half in range(2):
                                start = place(i * 2 + half, parity, b, a_lo)
                                sums[column // LANES, pl.ds(start, n_row, stride=RUN), :] = (
                                    halves[half][a_lo]
                                )
                        else:
                            both = jnp.concatenate([halves[0][a_lo], halves[1][a_lo]], axis=0)
                            mats[
                                operand,
                                pl.ds(pl.multiple_of(a_lo * tile + i * 16, 16), 16),
                                column : column + LANES,
                            ] = both.astype(BF16)
                    return 0

                lax.fori_loop(0, n_a // 2, step, 0)
        if scatter:
            for n in range(size // LANES):
                mats[operand, :, n * LANES : (n + 1) * LANES] = sums[n].astype(BF16)
    width = 2 * LANES
    for n in range(size // width):
        here = slice(n * width, (n + 1) * width)
        if outgoing:
            form, right = (((1,), (1,)), ((), ())), mats[1, here, :]
        else:
            form, right = (((0,), (0,)), ((), ())), mats[1, :, here]
        total = lax.dot_general(mats[0], right, form, preferred_element_type=F32)
        for j in range(2):
            sums[2 * n + j] = total[:, j * LANES : (j + 1) * LANES]
    for parity in range(2):
        for b in range(n_b):
            column = (parity * n_b + b) * LANES

            def leave(a, _, parity=parity, b=b, column=column):
                parts = []
                for a_lo in range(8):
                    if outgoing:
                        rows = pl.ds(pl.multiple_of(a_lo * tile + a * 8, 8), n_row)
                    else:
                        rows = pl.ds(place(a, parity, b, a_lo), n_row, stride=RUN)
                    parts.append(sums[column // LANES, rows, :])
                for c, part in enumerate(exchange(parts)):
                    flat_out[
                        pl.ds(
                            (2 * c + parity) * chunks + b * n_a + a, n_row, stride=n_col * chunks
                        ),
                        :,
                    ] = part
                return 0

            lax.fori_loop(0, n_a, leave, 0)
    pack(flat_out, out_ref)


def call(kernel, outs, scratch, *args):
    vmem = pl.BlockSpec(memory_space=pltpu.VMEM)
    many = isinstance(outs, (list, tuple))
    return pl.pallas_call(
        kernel,
        out_shape=outs,
        in_specs=[vmem] * len(args),
        out_specs=[vmem] * len(outs) if many else vmem,
        scratch_shapes=scratch,
        compiler_params=pltpu.CompilerParams(vmem_limit_bytes=56 << 20),
    )(*args)


def body(
    pair,
    residue_mask,
    out_ab_weight,
    out_gate_weight,
    out_z_weight,
    in_ab_weight,
    in_gate_weight,
    in_z_weight,
    trans_up,
    trans_down,
):
    n_row, n_col = lax.axis_size("row"), lax.axis_size("col")
    rows, cols, channels = pair.shape
    hidden = out_z_weight.shape[0]
    n_a, n_b = rows // SUB, cols // RUN
    chunks = n_a * n_b
    size = n_row * rows
    present = residue_mask.astype(F32)
    mask_rows = lax.dynamic_slice_in_dim(present, lax.axis_index("row") * rows, rows)
    mask_cols = lax.dynamic_slice_in_dim(present, lax.axis_index("col") * cols, cols)
    mask = (
        mask_rows.reshape(1, n_a, SUB, 1) * mask_cols.reshape(n_b, 1, 1, RUN)
    ).reshape(chunks, LANES)

    shape = jax.ShapeDtypeStruct
    operand_outs = [
        shape((hidden, 2 * chunks, LANES), BF16),
        shape((channels, chunks * LANES), F32),
        shape((channels, chunks * LANES), BF16),
    ]
    flat_two = pltpu.VMEM((hidden * 2 * chunks, LANES), F32)
    flat_one = pltpu.VMEM((hidden * chunks, LANES), F32)

    def move(x):
        return lax.all_to_all(x, AXES, 0, 0, tiled=True)

    def triangle(both, outgoing):
        return move(
            call(
                functools.partial(triangle_kernel, n_row, n_col, n_a, n_b, outgoing),
                shape((n_row * n_col, chunks, LANES), BF16),
                [flat_two, pltpu.VMEM((2, size, size), BF16), pltpu.VMEM((size // LANES, size, LANES), F32), flat_one],
                move(both),
            )
        )

    both, gating, current = call(
        first_kernel, operand_outs, [flat_two], pair, mask, out_ab_weight, out_gate_weight
    )
    sums = triangle(both, True)
    both, gating, current = call(
        middle_kernel, operand_outs, [flat_one, flat_two],
        sums, current, gating, mask, out_z_weight, in_ab_weight, in_gate_weight,
    )
    sums = triangle(both, False)
    return call(
        last_kernel, shape(pair.shape, pair.dtype), [flat_one],
        sums, current, gating, in_z_weight, trans_up, trans_down,
    )


def solution(mesh):
    placed = (P("row", "col", None), P(), P(), P(), P(), P(), P(), P(), P(), P())
    return jax.shard_map(
        body, mesh=mesh, in_specs=placed, out_specs=P("row", "col", None), check_vma=False
    )
```

```python
import functools

import jax
import jax.numpy as jnp
from jax import lax
from jax.experimental import pallas as pl
from jax.experimental.pallas import tpu as pltpu
from jax.sharding import PartitionSpec as P

EPS = 1e-05
AXES = ("row", "col")
LANES = 128
SUB = 8
RUN = 16
GROUP = 12
AT_ONCE = 12
BF16 = jnp.bfloat16
F32 = jnp.float32


def norm(x):
    center = x - jnp.mean(x, axis=0, keepdims=True)
    return center * lax.rsqrt(jnp.mean(center * center, axis=0, keepdims=True) + EPS)


def sigmoid(x):
    return 0.5 * jnp.tanh(0.5 * x) + 0.5


def dot(a, b):
    return jnp.dot(a, b, preferred_element_type=F32)


def turned(w_ref):
    return w_ref[...].astype(F32).T.astype(BF16)


def emit_operands(current, ab, gate, mask, chunk, chunks, flat, gating_ref):
    normed = norm(current).astype(BF16)
    hidden = ab.shape[0] // 4
    width = current.shape[1]
    p = dot(ab, normed)
    left = mask * sigmoid(p[hidden : 2 * hidden]) * p[:hidden]
    right = mask * sigmoid(p[3 * hidden :]) * p[2 * hidden : 3 * hidden]
    for j in range(width // LANES):
        lanes = slice(j * LANES, (j + 1) * LANES)
        flat[pl.ds(chunk + j, hidden, stride=2 * chunks), :] = left[:, lanes]
        flat[pl.ds(chunks + chunk + j, hidden, stride=2 * chunks), :] = right[:, lanes]
    here = pl.ds(pl.multiple_of(chunk * LANES, LANES), width)
    gating_ref[:, here] = sigmoid(dot(gate, normed))


def pack(flat, out_ref):
    n, rows = out_ref.shape[0], out_ref.shape[1]

    def step(i, _):
        out_ref[i] = flat[pl.ds(pl.multiple_of(i * rows, 4), rows), :].astype(out_ref.dtype)
        return 0

    lax.fori_loop(0, n, step, 0, unroll=8)


def unpack(in_ref, flat):
    n, rows = in_ref.shape[0], in_ref.shape[1]

    def step(i, _):
        flat[pl.ds(pl.multiple_of(i * rows, 4), rows), :] = in_ref[i].astype(F32)
        return 0

    lax.fori_loop(0, n, step, 0, unroll=8)


def group_mask(mask_ref, chunk):
    rows = [mask_ref[pl.ds(chunk + j, 1), :] for j in range(GROUP)]
    return jnp.concatenate(rows, axis=1)


def first_kernel(x_ref, mask_ref, ab_ref, gate_ref, out_ref, gating_ref, current_ref, flat):
    rows, cols, channels = x_ref.shape
    n_a, n_b = rows // SUB, cols // RUN
    chunks = n_a * n_b
    ab, gate = turned(ab_ref), turned(gate_ref)
    per = n_a // GROUP

    def step(g, _):
        b = g // per
        a = g % per
        block = x_ref[
            pl.ds(pl.multiple_of(a * GROUP * SUB, SUB), GROUP * SUB),
            pl.ds(pl.multiple_of(b * RUN, RUN), RUN),
            :,
        ]
        current = block.astype(F32).reshape(GROUP * LANES, channels).T
        here = pl.ds(pl.multiple_of(g * GROUP * LANES, LANES), GROUP * LANES)
        current_ref[:, here] = current.astype(BF16)
        chunk = g * GROUP
        emit_operands(
            current, ab, gate, group_mask(mask_ref, chunk), chunk, chunks, flat, gating_ref
        )
        return 0

    lax.fori_loop(0, chunks // GROUP, step, 0)
    pack(flat, out_ref)


def finish(flat_in, chunk, chunks, z, gating, current):
    channels = current.shape[0]
    triangle = jnp.concatenate(
        [flat_in[pl.ds(chunk + j, channels, stride=chunks), :] for j in range(GROUP)], axis=1
    )
    update = gating * dot(z, norm(triangle).astype(BF16))
    return (current.astype(F32) + update).astype(BF16)


def middle_kernel(
    t_ref, current_in, gating_in, mask_ref, z_ref, ab_ref, gate_ref,
    out_ref, gating_ref, current_ref, flat_in, flat,
):
    chunks = t_ref.shape[1]
    z, ab, gate = turned(z_ref), turned(ab_ref), turned(gate_ref)
    unpack(t_ref, flat_in)

    def step(g, _):
        chunk = g * GROUP
        here = pl.ds(pl.multiple_of(chunk * LANES, LANES), GROUP * LANES)
        current = finish(flat_in, chunk, chunks, z, gating_in[:, here], current_in[:, here])
        current_ref[:, here] = current
        emit_operands(
            current.astype(F32), ab, gate, group_mask(mask_ref, chunk), chunk, chunks, flat,
            gating_ref,
        )
        return 0

    lax.fori_loop(0, chunks // GROUP, step, 0)
    pack(flat, out_ref)


def last_kernel(
    t_ref, current_in, gating_in, z_ref, up_ref, down_ref, out_ref, flat_in
):
    chunks = t_ref.shape[1]
    rows, cols, channels = out_ref.shape
    per = (rows // SUB) // GROUP
    z, up, down = turned(z_ref), turned(up_ref), turned(down_ref)
    unpack(t_ref, flat_in)

    def step(g, _):
        chunk = g * GROUP
        here = pl.ds(pl.multiple_of(chunk * LANES, LANES), GROUP * LANES)
        current = finish(flat_in, chunk, chunks, z, gating_in[:, here], current_in[:, here])
        current = current.astype(F32)
        expanded = jnp.maximum(dot(up, norm(current).astype(BF16)), 0.0).astype(BF16)
        result = current + dot(down, expanded)
        b = g // per
        a = g % per
        out_ref[
            pl.ds(pl.multiple_of(a * GROUP * SUB, SUB), GROUP * SUB),
            pl.ds(pl.multiple_of(b * RUN, RUN), RUN),
            :,
        ] = result.T.reshape(GROUP * SUB, RUN, channels).astype(out_ref.dtype)
        return 0

    lax.fori_loop(0, chunks // GROUP, step, 0)


def exchange(parts):
    group = lax.broadcasted_iota(jnp.int32, parts[0].shape, 1) // RUN
    parts = list(parts)
    for bit in (1, 2, 4):
        chosen = (group // bit) % 2 == 1
        for i in range(8):
            if i & bit:
                continue
            low, high = parts[i], parts[i + bit]
            parts[i] = jnp.where(chosen, pltpu.roll(high, RUN * bit, 1), low)
            parts[i + bit] = jnp.where(chosen, high, pltpu.roll(low, LANES - RUN * bit, 1))
    return parts


def triangle_kernel(n_row, n_col, n_a, n_b, outgoing, in_ref, out_ref, flat, mats, sums, flat_out):
    chunks = n_a * n_b
    tile = n_row * n_a
    tiles = 2 * n_b
    unpack(in_ref, flat)

    def place(a, a_lo):
        t = a // (n_a // 2)
        rest = a % (n_a // 2)
        return t * (n_b * LANES) + (rest // 2) * LANES + (rest % 2) * SUB + a_lo

    def enter(operand, scatter, i):
        column = i // (n_a // AT_ONCE)
        parity, b = column // n_b, column % n_b
        first = (i % (n_a // AT_ONCE)) * AT_ONCE
        for pair in range(AT_ONCE // 2):
            parts = []
            for c in range(8):
                rows = [
                    flat[
                        pl.ds(
                            (2 * c + parity) * 2 * chunks
                            + operand * chunks + b * n_a + first + 2 * pair + half,
                            n_row,
                            stride=n_col * 2 * chunks,
                        ),
                        :,
                    ]
                    for half in range(2)
                ]
                parts.append(jnp.concatenate(rows, axis=0).astype(BF16))
            parts = exchange(parts)
            for a_lo in range(8):
                if scatter:
                    wide = parts[a_lo].astype(F32)
                    for half in range(2):
                        start = place(first + 2 * pair + half, a_lo)
                        sums[column, pl.ds(start, n_row, stride=RUN), :] = (
                            wide[half * n_row : (half + 1) * n_row]
                        )
                else:
                    start = a_lo * tile + (first + 2 * pair) * n_row
                    mats[operand, column, pl.ds(pl.multiple_of(start, 16), 16), :] = (
                        parts[a_lo]
                    )

    def loop(n, f):
        def step(i, _):
            f(i)
            return 0

        lax.fori_loop(0, n, step, 0)

    for operand in range(2):
        scatter = outgoing and operand == 1
        loop(tiles * n_a // AT_ONCE, functools.partial(enter, operand, scatter))
        if scatter:
            for n in range(tiles):
                mats[operand, n] = sums[n].astype(BF16)

    whole = jnp.concatenate([mats[0, n] for n in range(tiles)], axis=1)
    for n in range(tiles // 2):
        if outgoing:
            rows = slice(2 * n * LANES, (2 * n + 2) * LANES)
            right = jnp.concatenate([mats[1, k, rows] for k in range(tiles)], axis=1)
            form = (((1,), (1,)), ((), ()))
        else:
            right = jnp.concatenate([mats[1, 2 * n], mats[1, 2 * n + 1]], axis=1)
            form = (((0,), (0,)), ((), ()))
        total = lax.dot_general(whole, right, form, preferred_element_type=F32)
        for j in range(2):
            sums[2 * n + j] = total[:, j * LANES : (j + 1) * LANES]

    def leave(i):
        column = i // (n_a // AT_ONCE)
        parity, b = column // n_b, column % n_b
        first = (i % (n_a // AT_ONCE)) * AT_ONCE
        for pair in range(AT_ONCE // 2):
            a = first + 2 * pair
            parts = []
            for a_lo in range(8):
                if outgoing:
                    start = a_lo * tile + a * n_row
                    value = sums[column, pl.ds(pl.multiple_of(start, 16), 16), :]
                else:
                    value = jnp.concatenate(
                        [
                            sums[column, pl.ds(place(a + half, a_lo), n_row, stride=RUN), :]
                            for half in range(2)
                        ],
                        axis=0,
                    )
                parts.append(value.astype(BF16))
            for c, part in enumerate(exchange(parts)):
                wide = part.astype(F32)
                for half in range(2):
                    flat_out[
                        pl.ds(
                            (2 * c + parity) * chunks + b * n_a + a + half,
                            n_row,
                            stride=n_col * chunks,
                        ),
                        :,
                    ] = wide[half * n_row : (half + 1) * n_row]

    loop(tiles * n_a // AT_ONCE, leave)
    pack(flat_out, out_ref)


def call(kernel, outs, scratch, *args):
    vmem = pl.BlockSpec(memory_space=pltpu.VMEM)
    many = isinstance(outs, (list, tuple))
    return pl.pallas_call(
        kernel,
        out_shape=outs,
        in_specs=[vmem] * len(args),
        out_specs=[vmem] * len(outs) if many else vmem,
        scratch_shapes=scratch,
        compiler_params=pltpu.CompilerParams(vmem_limit_bytes=56 << 20),
    )(*args)


def body(
    pair,
    residue_mask,
    out_ab_weight,
    out_gate_weight,
    out_z_weight,
    in_ab_weight,
    in_gate_weight,
    in_z_weight,
    trans_up,
    trans_down,
):
    n_row, n_col = lax.axis_size("row"), lax.axis_size("col")
    rows, cols, channels = pair.shape
    hidden = out_z_weight.shape[0]
    n_a, n_b = rows // SUB, cols // RUN
    chunks = n_a * n_b
    size = n_row * rows
    present = residue_mask.astype(F32)
    mask_rows = lax.dynamic_slice_in_dim(present, lax.axis_index("row") * rows, rows)
    mask_cols = lax.dynamic_slice_in_dim(present, lax.axis_index("col") * cols, cols)
    mask = (
        mask_rows.reshape(1, n_a, SUB, 1) * mask_cols.reshape(n_b, 1, 1, RUN)
    ).reshape(chunks, LANES)

    shape = jax.ShapeDtypeStruct
    operand_outs = [
        shape((hidden, 2 * chunks, LANES), BF16),
        shape((channels, chunks * LANES), F32),
        shape((channels, chunks * LANES), BF16),
    ]
    flat_two = pltpu.VMEM((hidden * 2 * chunks, LANES), F32)
    flat_one = pltpu.VMEM((hidden * chunks, LANES), F32)

    def move(x):
        return lax.all_to_all(x, AXES, 0, 0, tiled=True)

    def triangle(both, outgoing):
        return move(
            call(
                functools.partial(triangle_kernel, n_row, n_col, n_a, n_b, outgoing),
                shape((n_row * n_col, chunks, LANES), BF16),
                [flat_two, pltpu.VMEM((2, size // LANES, size, LANES), BF16), pltpu.VMEM((size // LANES, size, LANES), F32), flat_one],
                move(both),
            )
        )

    both, gating, current = call(
        first_kernel, operand_outs, [flat_two], pair, mask, out_ab_weight, out_gate_weight
    )
    sums = triangle(both, True)
    both, gating, current = call(
        middle_kernel, operand_outs, [flat_one, flat_two],
        sums, current, gating, mask, out_z_weight, in_ab_weight, in_gate_weight,
    )
    sums = triangle(both, False)
    return call(
        last_kernel, shape(pair.shape, pair.dtype), [flat_one],
        sums, current, gating, in_z_weight, trans_up, trans_down,
    )


def solution(mesh):
    placed = (P("row", "col", None), P(), P(), P(), P(), P(), P(), P(), P(), P())
    return jax.shard_map(
        body, mesh=mesh, in_specs=placed, out_specs=P("row", "col", None), check_vma=False
    )
```

```python
import functools

import jax
import jax.numpy as jnp
from jax import lax
from jax.experimental import pallas as pl
from jax.experimental.pallas import tpu as pltpu
from jax.sharding import PartitionSpec as P

EPS = 1e-05
LANES = 128
SUB = 8
RUN = 16
BF16 = jnp.bfloat16
F32 = jnp.float32

SIZES = (4, 4, 8)
ORDERS = ((2, 1, 0), (1, 0, 2), (0, 2, 1))
MESH = pl.DeviceIdType.MESH


def norm(x):
    center = x - jnp.mean(x, axis=0, keepdims=True)
    return center * lax.rsqrt(jnp.mean(center * center, axis=0, keepdims=True) + EPS)


def sigmoid(x):
    return 0.5 * jnp.tanh(0.5 * x) + 0.5


def dot(a, b):
    return jnp.dot(a, b, preferred_element_type=F32)


def turned(w_ref):
    return w_ref[...].astype(F32).T.astype(BF16)


def exchange(parts):
    group = lax.broadcasted_iota(jnp.int32, parts[0].shape, 1) // RUN
    parts = list(parts)
    for bit in (1, 2, 4):
        chosen = (group // bit) % 2 == 1
        for i in range(8):
            if i & bit:
                continue
            low, high = parts[i], parts[i + bit]
            parts[i] = jnp.where(chosen, pltpu.roll(high, RUN * bit, 1), low)
            parts[i + bit] = jnp.where(chosen, high, pltpu.roll(low, LANES - RUN * bit, 1))
    return parts


def coordinates():
    row, col = lax.axis_index("row"), lax.axis_index("col")
    return row // 2, (row % 2) * 2 + (col // 2) % 2, (col // 4) * 2 + col % 2


def device(place):
    z, y, x = place
    return z * 2 + y // 2, (x // 2) * 4 + (y % 2) * 2 + x % 2


def loop(n, f, unroll=1):
    def step(i, _):
        f(i)
        return 0

    lax.fori_loop(0, n, step, 0, unroll=unroll)


def along(ref, axis, at):
    return ref.at[(slice(None),) * axis + (at,)]


class Move:
    def __init__(self, me, buffers, index, send, receive, local):
        self.me, self.buffers, self.index = me, buffers, index
        self.send, self.receive, self.local = send, receive, local

    def parts(self, third, stage):
        axis = ORDERS[third][stage]
        source, target = self.buffers[stage].at[third], self.buffers[stage + 1].at[third]
        return axis, source, target, (self.index, third, stage)

    def start(self, third, stage):
        axis, source, target, at = self.parts(third, stage)
        here = self.me[axis]
        for step in range(1, SIZES[axis]):
            there = (here + step) % SIZES[axis]
            place = list(self.me)
            place[axis] = there
            pltpu.make_async_remote_copy(
                src_ref=along(source, axis, there),
                dst_ref=along(target, axis, here),
                send_sem=self.send.at[at],
                recv_sem=self.receive.at[at],
                device_id=device(place),
                device_id_type=MESH,
            ).start()
        pltpu.make_async_copy(
            along(source, axis, here), along(target, axis, here), self.local.at[at]
        ).start()

    def arrive(self, third, stage):
        axis, source, target, at = self.parts(third, stage)
        most = along(target, axis, slice(1, SIZES[axis]))
        pltpu.make_async_copy(most, most, self.receive.at[at]).wait()
        one = along(target, axis, self.me[axis])
        pltpu.make_async_copy(one, one, self.local.at[at]).wait()

    def sent(self):
        for third in range(3):
            for stage in range(3):
                axis, source, target, at = self.parts(third, stage)
                most = along(source, axis, slice(1, SIZES[axis]))
                pltpu.make_async_copy(most, most, self.send.at[at]).wait()

    def advance(self):
        for stage in (1, 2):
            for third in range(3):
                self.arrive(third, stage - 1)
                self.start(third, stage)

    def at_third(self, third, act):
        for one in range(3):
            pl.when(third == one)(functools.partial(act, one))

    def begin(self, third):
        self.at_third(third, lambda one: self.start(one, 0))

    def end(self, third):
        self.at_third(third, lambda one: self.arrive(one, 2))


def put(flat, buffer, third, by_device):
    rows = buffer.shape[4]

    def one(i):
        place = (i // 32, (i // 8) % 4, i % 8)
        first = i
        if by_device:
            row, col = device(place)
            first = row * 16 + col
        buffer[(third,) + place] = flat[pl.ds(pl.multiple_of(first * rows, 4), rows), :].astype(
            BF16
        )

    loop(128, one, 8)


def take(buffer, flat, third, by_device):
    rows = buffer.shape[4]

    def one(i):
        place = (i // 32, (i // 8) % 4, i % 8)
        first = i
        if by_device:
            row, col = device(place)
            first = row * 16 + col
        flat[pl.ds(pl.multiple_of(first * rows, 4), rows), :] = buffer[(third,) + place].astype(F32)

    loop(128, one, 8)


def kernel(
    x_ref, mask_ref, ab1_ref, gate1_ref, z1_ref, ab2_ref, gate2_ref, z2_ref, up_ref, down_ref,
    out_ref,
    current_ref, gating_ref, flat_two, flat_one, mats, sums,
    p0, p1, p2, p3, q0, q1, q2, q3, r0, r1, r2, r3, s0, s1, s2, s3,
    send, receive, local,
):
    n_row, n_col = 8, 16
    rows, cols, channels = x_ref.shape
    n_a, n_b = rows // SUB, cols // RUN
    width = n_a * LANES
    tile = n_row * n_a
    tiles = 2 * n_b
    me = coordinates()
    moves = [
        Move(me, buffers, index, send, receive, local)
        for index, buffers in enumerate(
            ((p0, p1, p2, p3), (q0, q1, q2, q3), (r0, r1, r2, r3), (s0, s1, s2, s3))
        )
    ]

    barrier = pltpu.get_barrier_semaphore()
    for axis in range(3):
        for step in range(1, SIZES[axis]):
            place = list(me)
            place[axis] = (me[axis] + step) % SIZES[axis]
            pl.semaphore_signal(barrier, inc=1, device_id=device(place), device_id_type=MESH)

    def lanes_of(third):
        return pl.ds(pl.multiple_of(third * width, LANES), width)

    def emit(third, current, ab, gate, move):
        normed = norm(current).astype(BF16)
        hidden = ab.shape[0] // 4
        mask = jnp.concatenate([mask_ref[pl.ds(third * n_a + j, 1), :] for j in range(n_a)], axis=1)
        p = dot(ab, normed)
        left = mask * sigmoid(p[hidden : 2 * hidden]) * p[:hidden]
        right = mask * sigmoid(p[3 * hidden :]) * p[2 * hidden : 3 * hidden]
        for j in range(n_a):
            lanes = slice(j * LANES, (j + 1) * LANES)
            flat_two[pl.ds(j, hidden, stride=2 * n_a), :] = left[:, lanes]
            flat_two[pl.ds(n_a + j, hidden, stride=2 * n_a), :] = right[:, lanes]
        gating_ref[:, lanes_of(third)] = sigmoid(dot(gate, normed))
        put(flat_two, move.buffers[0], third, False)

    def finish(third, z, move):
        take(move.buffers[3], flat_one, third, False)
        triangle = jnp.concatenate(
            [flat_one[pl.ds(j, channels, stride=n_a), :] for j in range(n_a)], axis=1
        )
        here = lanes_of(third)
        update = gating_ref[:, here] * dot(z, norm(triangle).astype(BF16))
        return (current_ref[:, here].astype(F32) + update).astype(BF16)

    def place_of(a, a_lo):
        t = a // (n_a // 2)
        rest = a % (n_a // 2)
        return t * (n_b * LANES) + (rest // 2) * LANES + (rest % 2) * SUB + a_lo

    def triangle(outgoing, inward, outward):
        def enter(third):
            inward.end(third)
            take(inward.buffers[3], flat_two, third, True)
            for operand in range(2):
                scatter = outgoing and operand == 1

                def one(parity, operand=operand, scatter=scatter):
                    column = parity * n_b + third
                    for a in range(0, n_a, 2):
                        parts = []
                        for c in range(8):
                            pieces = [
                                flat_two[
                                    pl.ds(
                                        (2 * c + parity) * 2 * n_a + operand * n_a + a + half,
                                        n_row,
                                        stride=n_col * 2 * n_a,
                                    ),
                                    :,
                                ]
                                for half in range(2)
                            ]
                            parts.append(jnp.concatenate(pieces, axis=0).astype(BF16))
                        parts = exchange(parts)
                        for a_lo in range(8):
                            if scatter:
                                wide = parts[a_lo].astype(F32)
                                for half in range(2):
                                    start = place_of(a + half, a_lo)
                                    sums[column, pl.ds(start, n_row, stride=RUN), :] = (
                                        wide[half * n_row : (half + 1) * n_row]
                                    )
                            else:
                                start = a_lo * tile + a * n_row
                                mats[operand, column, pl.ds(start, 16), :] = parts[a_lo]
                    if scatter:
                        mats[operand, column] = sums[column].astype(BF16)

                loop(2, one)

        loop(n_b, enter)
        whole = jnp.concatenate([mats[0, n] for n in range(tiles)], axis=1)
        for n in range(tiles // 2):
            if outgoing:
                here = slice(2 * n * LANES, (2 * n + 2) * LANES)
                right = jnp.concatenate([mats[1, k, here] for k in range(tiles)], axis=1)
                form = (((1,), (1,)), ((), ()))
            else:
                right = jnp.concatenate([mats[1, 2 * n], mats[1, 2 * n + 1]], axis=1)
                form = (((0,), (0,)), ((), ()))
            total = lax.dot_general(whole, right, form, preferred_element_type=F32)
            for j in range(2):
                sums[2 * n + j] = total[:, j * LANES : (j + 1) * LANES]

        def leave(third):
            def one(parity):
                column = parity * n_b + third
                for a in range(0, n_a, 2):
                    parts = []
                    for a_lo in range(8):
                        if outgoing:
                            value = sums[column, pl.ds(a_lo * tile + a * n_row, 16), :]
                        else:
                            value = jnp.concatenate(
                                [
                                    sums[column, pl.ds(place_of(a + half, a_lo), n_row, stride=RUN), :]
                                    for half in range(2)
                                ],
                                axis=0,
                            )
                        parts.append(value.astype(BF16))
                    for c, part in enumerate(exchange(parts)):
                        wide = part.astype(F32)
                        for half in range(2):
                            flat_one[
                                pl.ds(
                                    (2 * c + parity) * n_a + a + half, n_row, stride=n_col * n_a
                                ),
                                :,
                            ] = wide[half * n_row : (half + 1) * n_row]

            loop(2, one)
            put(flat_one, outward.buffers[0], third, True)
            outward.begin(third)

        loop(n_b, leave)

    ab, gate = turned(ab1_ref), turned(gate1_ref)

    def first(third):
        block = x_ref[:, pl.ds(pl.multiple_of(third * RUN, RUN), RUN), :]
        current = block.astype(F32).reshape(width, channels).T
        current_ref[:, lanes_of(third)] = current.astype(BF16)
        emit(third, current, ab, gate, moves[0])
        pl.when(third == 0)(lambda: pl.semaphore_wait(barrier, sum(SIZES) - 3))
        moves[0].begin(third)

    loop(n_b, first)
    moves[0].advance()
    triangle(True, moves[0], moves[1])

    z, ab2, gate2 = turned(z1_ref), turned(ab2_ref), turned(gate2_ref)
    moves[1].advance()

    def middle(third):
        moves[1].end(third)
        current = finish(third, z, moves[1])
        current_ref[:, lanes_of(third)] = current
        emit(third, current.astype(F32), ab2, gate2, moves[2])
        moves[2].begin(third)

    loop(n_b, middle)
    moves[2].advance()
    triangle(False, moves[2], moves[3])

    z2, up, down = turned(z2_ref), turned(up_ref), turned(down_ref)
    moves[3].advance()

    def last(third):
        moves[3].end(third)
        current = finish(third, z2, moves[3]).astype(F32)
        expanded = jnp.maximum(dot(up, norm(current).astype(BF16)), 0.0).astype(BF16)
        result = current + dot(down, expanded)
        out_ref[:, pl.ds(pl.multiple_of(third * RUN, RUN), RUN), :] = result.T.reshape(
            rows, RUN, channels
        ).astype(out_ref.dtype)

    loop(n_b, last)
    for move in moves:
        move.sent()


def body(
    pair,
    residue_mask,
    out_ab_weight,
    out_gate_weight,
    out_z_weight,
    in_ab_weight,
    in_gate_weight,
    in_z_weight,
    trans_up,
    trans_down,
):
    rows, cols, channels = pair.shape
    n_a, n_b = rows // SUB, cols // RUN
    chunks = n_a * n_b
    size = 8 * rows
    present = residue_mask.astype(F32)
    mask_rows = lax.dynamic_slice_in_dim(present, lax.axis_index("row") * rows, rows)
    mask_cols = lax.dynamic_slice_in_dim(present, lax.axis_index("col") * cols, cols)
    mask = (
        mask_rows.reshape(1, n_a, SUB, 1) * mask_cols.reshape(n_b, 1, 1, RUN)
    ).reshape(chunks, LANES)
    vmem = pl.BlockSpec(memory_space=pltpu.VMEM)
    two = pltpu.VMEM((n_b,) + SIZES + (2 * n_a, LANES), BF16)
    one = pltpu.VMEM((n_b,) + SIZES + (n_a, LANES), BF16)
    return pl.pallas_call(
        kernel,
        out_shape=jax.ShapeDtypeStruct(pair.shape, pair.dtype),
        in_specs=[vmem] * 10,
        out_specs=vmem,
        scratch_shapes=[
            pltpu.VMEM((channels, chunks * LANES), BF16),
            pltpu.VMEM((channels, chunks * LANES), F32),
            pltpu.VMEM((128 * 2 * n_a, LANES), F32),
            pltpu.VMEM((128 * n_a, LANES), F32),
            pltpu.VMEM((2, size // LANES, size, LANES), BF16),
            pltpu.VMEM((size // LANES, size, LANES), F32),
            *([two] * 4 + [one] * 4) * 2,
            pltpu.SemaphoreType.DMA((4, 3, 3)),
            pltpu.SemaphoreType.DMA((4, 3, 3)),
            pltpu.SemaphoreType.DMA((4, 3, 3)),
        ],
        compiler_params=pltpu.CompilerParams(
            collective_id=0, has_side_effects=True, vmem_limit_bytes=60 << 20
        ),
    )(
        pair, mask, out_ab_weight, out_gate_weight, out_z_weight, in_ab_weight, in_gate_weight,
        in_z_weight, trans_up, trans_down,
    )


def solution(mesh):
    placed = (P("row", "col", None), P(), P(), P(), P(), P(), P(), P(), P(), P())
    return jax.shard_map(
        body, mesh=mesh, in_specs=placed, out_specs=P("row", "col", None), check_vma=False
    )
```

```python
import functools

import jax
import jax.numpy as jnp
from jax import lax
from jax.experimental import pallas as pl
from jax.experimental.pallas import tpu as pltpu
from jax.sharding import PartitionSpec as P

EPS = 1e-05
LANES = 128
SUB = 8
RUN = 16
BF16 = jnp.bfloat16
F32 = jnp.float32

SIZES = (16, 8)
ORDERS = ((1, 0), (0, 1), (1, 0))
STAGES = 2
MESH = pl.DeviceIdType.MESH


def norm(x):
    center = x - jnp.mean(x, axis=0, keepdims=True)
    return center * lax.rsqrt(jnp.mean(center * center, axis=0, keepdims=True) + EPS)


def sigmoid(x):
    return 0.5 * jnp.tanh(0.5 * x) + 0.5


def dot(a, b):
    return jnp.dot(a, b, preferred_element_type=F32)


def turned(w_ref):
    return w_ref[...].astype(F32).T.astype(BF16)


def exchange(parts):
    group = lax.broadcasted_iota(jnp.int32, parts[0].shape, 1) // RUN
    parts = list(parts)
    for bit in (1, 2, 4):
        chosen = (group // bit) % 2 == 1
        for i in range(8):
            if i & bit:
                continue
            low, high = parts[i], parts[i + bit]
            parts[i] = jnp.where(chosen, pltpu.roll(high, RUN * bit, 1), low)
            parts[i + bit] = jnp.where(chosen, high, pltpu.roll(low, LANES - RUN * bit, 1))
    return parts


def coordinates():
    row, col = lax.axis_index("row"), lax.axis_index("col")
    return row * 2 + (col // 2) % 2, (col // 4) * 2 + col % 2


def device(place):
    plane, x = place
    return plane // 2, (x // 2) * 4 + (plane % 2) * 2 + x % 2


def loop(n, f, unroll=1):
    def step(i, _):
        f(i)
        return 0

    lax.fori_loop(0, n, step, 0, unroll=unroll)


def along(ref, axis, at):
    return ref.at[(slice(None),) * axis + (at,)]


class Move:
    def __init__(self, me, buffers, index, send, receive, local):
        self.me, self.buffers, self.index = me, buffers, index
        self.send, self.receive, self.local = send, receive, local

    def parts(self, third, stage):
        axis = ORDERS[third][stage]
        source, target = self.buffers[stage].at[third], self.buffers[stage + 1].at[third]
        return axis, source, target, (self.index, third, stage)

    def start(self, third, stage):
        axis, source, target, at = self.parts(third, stage)
        here = self.me[axis]
        for step in range(1, SIZES[axis]):
            there = (here + step) % SIZES[axis]
            place = list(self.me)
            place[axis] = there
            pltpu.make_async_remote_copy(
                src_ref=along(source, axis, there),
                dst_ref=along(target, axis, here),
                send_sem=self.send.at[at],
                recv_sem=self.receive.at[at],
                device_id=device(place),
                device_id_type=MESH,
            ).start()
        pltpu.make_async_copy(
            along(source, axis, here), along(target, axis, here), self.local.at[at]
        ).start()

    def arrive(self, third, stage):
        axis, source, target, at = self.parts(third, stage)
        most = along(target, axis, slice(1, SIZES[axis]))
        pltpu.make_async_copy(most, most, self.receive.at[at]).wait()
        one = along(target, axis, self.me[axis])
        pltpu.make_async_copy(one, one, self.local.at[at]).wait()

    def sent(self):
        for third in range(3):
            for stage in range(STAGES):
                axis, source, target, at = self.parts(third, stage)
                most = along(source, axis, slice(1, SIZES[axis]))
                pltpu.make_async_copy(most, most, self.send.at[at]).wait()

    def advance(self):
        for stage in range(1, STAGES):
            for third in range(3):
                self.arrive(third, stage - 1)
                self.start(third, stage)

    def at_third(self, third, act):
        for one in range(3):
            pl.when(third == one)(functools.partial(act, one))

    def begin(self, third):
        self.at_third(third, lambda one: self.start(one, 0))

    def end(self, third):
        self.at_third(third, lambda one: self.arrive(one, STAGES - 1))


def put(flat, buffer, third):
    planes, places, rows = buffer.shape[1:4]

    def one(plane):
        block = flat[pl.ds(pl.multiple_of(plane * places * rows, 8), places * rows), :]
        for x in range(places):
            buffer[third, plane, x] = block[x * rows : (x + 1) * rows].astype(BF16)

    loop(planes, one, 2)


def take(buffer, flat, third):
    planes, places, rows = buffer.shape[1:4]

    def one(plane):
        block = [buffer[third, plane, x].astype(F32) for x in range(places)]
        flat[pl.ds(pl.multiple_of(plane * places * rows, 8), places * rows), :] = jnp.concatenate(
            block, axis=0
        )

    loop(planes, one, 2)


def kernel(
    x_ref, mask_ref, ab1_ref, gate1_ref, z1_ref, ab2_ref, gate2_ref, z2_ref, up_ref, down_ref,
    out_ref,
    current_ref, gating_ref, flat_two, flat_one, mats, sums,
    p0, p1, p2, q0, q1, q2, r0, r1, r2, s0, s1, s2,
    send, receive, local,
):
    n_row, n_col = 8, 16
    rows, cols, channels = x_ref.shape
    n_a, n_b = rows // SUB, cols // RUN
    width = n_a * LANES
    tile = n_row * n_a
    tiles = 2 * n_b
    me = coordinates()
    moves = [
        Move(me, buffers, index, send, receive, local)
        for index, buffers in enumerate(
            ((p0, p1, p2), (q0, q1, q2), (r0, r1, r2), (s0, s1, s2))
        )
    ]

    barrier = pltpu.get_barrier_semaphore()
    for axis in range(len(SIZES)):
        for step in range(1, SIZES[axis]):
            place = list(me)
            place[axis] = (me[axis] + step) % SIZES[axis]
            pl.semaphore_signal(barrier, inc=1, device_id=device(place), device_id_type=MESH)

    def lanes_of(third):
        return pl.ds(pl.multiple_of(third * width, LANES), width)

    def emit(third, current, ab, gate, move):
        normed = norm(current).astype(BF16)
        hidden = ab.shape[0] // 4
        mask = jnp.concatenate([mask_ref[pl.ds(third * n_a + j, 1), :] for j in range(n_a)], axis=1)
        p = dot(ab, normed)
        left = mask * sigmoid(p[hidden : 2 * hidden]) * p[:hidden]
        right = mask * sigmoid(p[3 * hidden :]) * p[2 * hidden : 3 * hidden]
        for j in range(n_a):
            lanes = slice(j * LANES, (j + 1) * LANES)
            flat_two[pl.ds(j, hidden, stride=2 * n_a), :] = left[:, lanes]
            flat_two[pl.ds(n_a + j, hidden, stride=2 * n_a), :] = right[:, lanes]
        gating_ref[:, lanes_of(third)] = sigmoid(dot(gate, normed))
        put(flat_two, move.buffers[0], third)

    def finish(third, z, move):
        take(move.buffers[STAGES], flat_one, third)
        triangle = jnp.concatenate(
            [flat_one[pl.ds(j, channels, stride=n_a), :] for j in range(n_a)], axis=1
        )
        here = lanes_of(third)
        update = gating_ref[:, here] * dot(z, norm(triangle).astype(BF16))
        return (current_ref[:, here].astype(F32) + update).astype(BF16)

    def place_of(a, a_lo):
        t = a // (n_a // 2)
        rest = a % (n_a // 2)
        return t * (n_b * LANES) + (rest // 2) * LANES + (rest % 2) * SUB + a_lo

    def place_at(c):
        return (c % 2) * 8 + (c // 2) * 2

    def triangle(outgoing, inward, outward):
        def enter(third):
            inward.end(third)
            take(inward.buffers[STAGES], flat_two, third)
            for operand in range(2):
                scatter = outgoing and operand == 1

                def one(parity, operand=operand, scatter=scatter):
                    column = parity * n_b + third
                    for a in range(0, n_a, 2):
                        parts = []
                        for c in range(8):
                            pieces = [
                                flat_two[
                                    pl.ds(
                                        (place_at(c) + parity) * 2 * n_a + operand * n_a + a + half,
                                        n_row,
                                        stride=n_col * 2 * n_a,
                                    ),
                                    :,
                                ]
                                for half in range(2)
                            ]
                            parts.append(jnp.concatenate(pieces, axis=0).astype(BF16))
                        parts = exchange(parts)
                        for a_lo in range(8):
                            if scatter:
                                wide = parts[a_lo].astype(F32)
                                for half in range(2):
                                    start = place_of(a + half, a_lo)
                                    sums[column, pl.ds(start, n_row, stride=RUN), :] = (
                                        wide[half * n_row : (half + 1) * n_row]
                                    )
                            else:
                                start = a_lo * tile + a * n_row
                                mats[operand, column, pl.ds(start, 16), :] = parts[a_lo]
                    if scatter:
                        mats[operand, column] = sums[column].astype(BF16)

                loop(2, one)

        loop(n_b, enter)
        whole = jnp.concatenate([mats[0, n] for n in range(tiles)], axis=1)
        for n in range(tiles // 2):
            if outgoing:
                here = slice(2 * n * LANES, (2 * n + 2) * LANES)
                right = jnp.concatenate([mats[1, k, here] for k in range(tiles)], axis=1)
                form = (((1,), (1,)), ((), ()))
            else:
                right = jnp.concatenate([mats[1, 2 * n], mats[1, 2 * n + 1]], axis=1)
                form = (((0,), (0,)), ((), ()))
            total = lax.dot_general(whole, right, form, preferred_element_type=F32)
            for j in range(2):
                sums[2 * n + j] = total[:, j * LANES : (j + 1) * LANES]

        def leave(third):
            def one(parity):
                column = parity * n_b + third
                for a in range(0, n_a, 2):
                    parts = []
                    for a_lo in range(8):
                        if outgoing:
                            value = sums[column, pl.ds(a_lo * tile + a * n_row, 16), :]
                        else:
                            value = jnp.concatenate(
                                [
                                    sums[column, pl.ds(place_of(a + half, a_lo), n_row, stride=RUN), :]
                                    for half in range(2)
                                ],
                                axis=0,
                            )
                        parts.append(value.astype(BF16))
                    for c, part in enumerate(exchange(parts)):
                        wide = part.astype(F32)
                        for half in range(2):
                            flat_one[
                                pl.ds(
                                    (place_at(c) + parity) * n_a + a + half,
                                    n_row,
                                    stride=n_col * n_a,
                                ),
                                :,
                            ] = wide[half * n_row : (half + 1) * n_row]

            loop(2, one)
            put(flat_one, outward.buffers[0], third)
            outward.begin(third)

        loop(n_b, leave)

    ab, gate = turned(ab1_ref), turned(gate1_ref)

    def first(third):
        block = x_ref[:, pl.ds(pl.multiple_of(third * RUN, RUN), RUN), :]
        current = block.astype(F32).reshape(width, channels).T
        current_ref[:, lanes_of(third)] = current.astype(BF16)
        emit(third, current, ab, gate, moves[0])
        pl.when(third == 0)(lambda: pl.semaphore_wait(barrier, sum(SIZES) - len(SIZES)))
        moves[0].begin(third)

    loop(n_b, first)
    moves[0].advance()
    triangle(True, moves[0], moves[1])

    z, ab2, gate2 = turned(z1_ref), turned(ab2_ref), turned(gate2_ref)
    moves[1].advance()

    def middle(third):
        moves[1].end(third)
        current = finish(third, z, moves[1])
        current_ref[:, lanes_of(third)] = current
        emit(third, current.astype(F32), ab2, gate2, moves[2])
        moves[2].begin(third)

    loop(n_b, middle)
    moves[2].advance()
    triangle(False, moves[2], moves[3])

    z2, up, down = turned(z2_ref), turned(up_ref), turned(down_ref)
    moves[3].advance()

    def last(third):
        moves[3].end(third)
        current = finish(third, z2, moves[3]).astype(F32)
        expanded = jnp.maximum(dot(up, norm(current).astype(BF16)), 0.0).astype(BF16)
        result = current + dot(down, expanded)
        out_ref[:, pl.ds(pl.multiple_of(third * RUN, RUN), RUN), :] = result.T.reshape(
            rows, RUN, channels
        ).astype(out_ref.dtype)

    loop(n_b, last)
    for move in moves:
        move.sent()


def body(
    pair,
    residue_mask,
    out_ab_weight,
    out_gate_weight,
    out_z_weight,
    in_ab_weight,
    in_gate_weight,
    in_z_weight,
    trans_up,
    trans_down,
):
    rows, cols, channels = pair.shape
    n_a, n_b = rows // SUB, cols // RUN
    chunks = n_a * n_b
    size = 8 * rows
    present = residue_mask.astype(F32)
    mask_rows = lax.dynamic_slice_in_dim(present, lax.axis_index("row") * rows, rows)
    mask_cols = lax.dynamic_slice_in_dim(present, lax.axis_index("col") * cols, cols)
    mask = (
        mask_rows.reshape(1, n_a, SUB, 1) * mask_cols.reshape(n_b, 1, 1, RUN)
    ).reshape(chunks, LANES)
    vmem = pl.BlockSpec(memory_space=pltpu.VMEM)
    two = pltpu.VMEM((n_b,) + SIZES + (2 * n_a, LANES), BF16)
    one = pltpu.VMEM((n_b,) + SIZES + (n_a, LANES), BF16)
    return pl.pallas_call(
        kernel,
        out_shape=jax.ShapeDtypeStruct(pair.shape, pair.dtype),
        in_specs=[vmem] * 10,
        out_specs=vmem,
        scratch_shapes=[
            pltpu.VMEM((channels, chunks * LANES), BF16),
            pltpu.VMEM((channels, chunks * LANES), F32),
            pltpu.VMEM((128 * 2 * n_a, LANES), F32),
            pltpu.VMEM((128 * n_a, LANES), F32),
            pltpu.VMEM((2, size // LANES, size, LANES), BF16),
            pltpu.VMEM((size // LANES, size, LANES), F32),
            *([two] * (STAGES + 1) + [one] * (STAGES + 1)) * 2,
            pltpu.SemaphoreType.DMA((4, 3, STAGES)),
            pltpu.SemaphoreType.DMA((4, 3, STAGES)),
            pltpu.SemaphoreType.DMA((4, 3, STAGES)),
        ],
        compiler_params=pltpu.CompilerParams(
            collective_id=0, has_side_effects=True, vmem_limit_bytes=60 << 20
        ),
    )(
        pair, mask, out_ab_weight, out_gate_weight, out_z_weight, in_ab_weight, in_gate_weight,
        in_z_weight, trans_up, trans_down,
    )


def solution(mesh):
    placed = (P("row", "col", None), P(), P(), P(), P(), P(), P(), P(), P(), P())
    return jax.shard_map(
        body, mesh=mesh, in_specs=placed, out_specs=P("row", "col", None), check_vma=False
    )
```

```python
import functools

import jax
import jax.numpy as jnp
from jax import lax
from jax.experimental import pallas as pl
from jax.experimental.pallas import tpu as pltpu
from jax.sharding import PartitionSpec as P

EPS = 1e-05
LANES = 128
SUB = 8
RUN = 16
BF16 = jnp.bfloat16
F32 = jnp.float32

SIZES = (16, 8)
STAGES = 2
FULL = 8
WHOLE = 4
GROUPS = 5
MESH = pl.DeviceIdType.MESH


def norm(x):
    center = x - jnp.mean(x, axis=0, keepdims=True)
    return center * lax.rsqrt(jnp.mean(center * center, axis=0, keepdims=True) + EPS)


def sigmoid(x):
    return 0.5 * jnp.tanh(0.5 * x) + 0.5


def dot(a, b):
    return jnp.dot(a, b, preferred_element_type=F32)


def turned(w_ref):
    return w_ref[...].astype(F32).T.astype(BF16)


def exchange(parts):
    group = lax.broadcasted_iota(jnp.int32, parts[0].shape, 1) // RUN
    parts = list(parts)
    for bit in (1, 2, 4):
        chosen = (group // bit) % 2 == 1
        for i in range(8):
            if i & bit:
                continue
            low, high = parts[i], parts[i + bit]
            parts[i] = jnp.where(chosen, pltpu.roll(high, RUN * bit, 1), low)
            parts[i + bit] = jnp.where(chosen, high, pltpu.roll(low, LANES - RUN * bit, 1))
    return parts


def coordinates():
    row, col = lax.axis_index("row"), lax.axis_index("col")
    return row * 2 + (col // 2) % 2, (col // 4) * 2 + col % 2


def device(place):
    plane, x = place
    return plane // 2, (x // 2) * 4 + (plane % 2) * 2 + x % 2


def loop(n, f, unroll=1):
    def step(i, _):
        f(i)
        return 0

    lax.fori_loop(0, n, step, 0, unroll=unroll)


def along(ref, axis, at):
    return ref.at[(slice(None),) * axis + (at,)]


class Move:
    def __init__(self, me, buffers, index, send, receive, local):
        self.me, self.buffers, self.index = me, buffers, index
        self.send, self.receive, self.local = send, receive, local

    def parts(self, group, stage):
        axis = (stage + 1 + group) % 2
        source, target = [
            whole.at[group] if group < WHOLE else last.at[0]
            for whole, last in self.buffers[stage : stage + 2]
        ]
        return axis, source, target, (self.index, group, stage)

    def start(self, group, stage):
        axis, source, target, at = self.parts(group, stage)
        here = self.me[axis]
        for step in range(1, SIZES[axis]):
            there = (here + step) % SIZES[axis]
            place = list(self.me)
            place[axis] = there
            pltpu.make_async_remote_copy(
                src_ref=along(source, axis, there),
                dst_ref=along(target, axis, here),
                send_sem=self.send.at[at],
                recv_sem=self.receive.at[at],
                device_id=device(place),
                device_id_type=MESH,
            ).start()
        pltpu.make_async_copy(
            along(source, axis, here), along(target, axis, here), self.local.at[at]
        ).start()

    def arrive(self, group, stage):
        axis, source, target, at = self.parts(group, stage)
        most = along(target, axis, slice(1, SIZES[axis]))
        pltpu.make_async_copy(most, most, self.receive.at[at]).wait()
        one = along(target, axis, self.me[axis])
        pltpu.make_async_copy(one, one, self.local.at[at]).wait()

    def sent(self):
        for group in range(GROUPS):
            for stage in range(STAGES):
                axis, source, target, at = self.parts(group, stage)
                most = along(source, axis, slice(1, SIZES[axis]))
                pltpu.make_async_copy(most, most, self.send.at[at]).wait()

    def advance(self):
        for group in range(GROUPS):
            self.arrive(group, 0)
            self.start(group, 1)

    def at_group(self, group, act):
        if isinstance(group, int):
            act(group)
            return
        for one in range(GROUPS):
            pl.when(group == one)(functools.partial(act, one))

    def begin(self, group):
        self.at_group(group, lambda one: self.start(one, 0))

    def end(self, group):
        self.at_group(group, lambda one: self.arrive(one, 1))


def spans(rows):
    return [(n * FULL, n * FULL + FULL // 2) for n in range(rows // FULL)]


def put(flat, buffers, group, short):
    whole, last = buffers
    planes, places, rows = whole.shape[1:4]

    def one(plane):
        block = flat[pl.ds(pl.multiple_of(plane * places * rows, 8), places * rows), :]
        for x in range(places):
            part = block[x * rows : (x + 1) * rows]
            if short:
                part = jnp.concatenate([part[i:j] for i, j in spans(rows)], axis=0)
                last[0, plane, x] = part.astype(BF16)
            else:
                whole[group, plane, x] = part.astype(BF16)

    loop(planes, one, 2)


def take(buffers, flat, group, short):
    whole, last = buffers
    planes, places, rows = whole.shape[1:4]

    def one(plane):
        first = pl.multiple_of(plane * places * rows, 8)
        if short:
            for x in range(places):
                part = last[0, plane, x].astype(F32)
                for n, (i, j) in enumerate(spans(rows)):
                    flat[pl.ds(first + (x * rows + i), j - i), :] = part[n * (j - i) : (n + 1) * (j - i)]
        else:
            block = [whole[group, plane, x].astype(F32) for x in range(places)]
            flat[pl.ds(first, places * rows), :] = jnp.concatenate(block, axis=0)

    loop(planes, one, 2)


def kernel(
    x_ref, mask_ref, ab1_ref, gate1_ref, z1_ref, ab2_ref, gate2_ref, z2_ref, up_ref, down_ref,
    out_ref,
    current_ref, gating_ref, flat_two, flat_one, mats, left_t, sums, *rest,
):
    n_row, n_col = 8, 16
    rows, cols, channels = x_ref.shape
    n_a, n_b = rows // SUB, cols // RUN
    tile = n_row * n_a
    tiles = 2 * n_b
    half = FULL // 2
    me = coordinates()
    buffers, (send, receive, local) = rest[:-3], rest[-3:]
    moves = []
    for index in range(4):
        mine = buffers[index * 6 : index * 6 + 6]
        pairs = [mine[i : i + 2] for i in range(0, 6, 2)]
        moves.append(Move(me, pairs, index, send, receive, local))

    barrier = pltpu.get_barrier_semaphore()
    for axis in range(len(SIZES)):
        for step in range(1, SIZES[axis]):
            place = list(me)
            place[axis] = (me[axis] + step) % SIZES[axis]
            pl.semaphore_signal(barrier, inc=1, device_id=device(place), device_id_type=MESH)

    def each_group(f):
        loop(WHOLE, lambda group: f(group, FULL))
        f(WHOLE, half)

    def lanes_of(group, count):
        return pl.ds(pl.multiple_of(group * (FULL * LANES), LANES), count * LANES)

    def blocks_of(group, count):
        found = []
        for i in range(count // half):
            number = group * 2 + i
            b, a = number // (n_a // half), number % (n_a // half)
            found.append(
                (
                    pl.ds(pl.multiple_of(a * (half * SUB), half * SUB), half * SUB),
                    pl.ds(pl.multiple_of(b * RUN, RUN), RUN),
                )
            )
        return found

    def emit(group, count, current, ab, gate, move):
        normed = norm(current).astype(BF16)
        hidden = ab.shape[0] // 4
        mask = jnp.concatenate(
            [mask_ref[pl.ds(group * FULL + j, 1), :] for j in range(count)], axis=1
        )
        p = dot(ab, normed)
        left = mask * sigmoid(p[hidden : 2 * hidden]) * p[:hidden]
        right = mask * sigmoid(p[3 * hidden :]) * p[2 * hidden : 3 * hidden]
        for j in range(count):
            lanes = slice(j * LANES, (j + 1) * LANES)
            flat_two[pl.ds(j, hidden, stride=2 * FULL), :] = left[:, lanes]
            flat_two[pl.ds(FULL + j, hidden, stride=2 * FULL), :] = right[:, lanes]
        gating_ref[:, lanes_of(group, count)] = sigmoid(dot(gate, normed))
        put(flat_two, move.buffers[0], group, count < FULL)

    def finish(group, count, z, move):
        take(move.buffers[STAGES], flat_one, group, count < FULL)
        triangle = jnp.concatenate(
            [flat_one[pl.ds(j, channels, stride=FULL), :] for j in range(count)], axis=1
        )
        here = lanes_of(group, count)
        update = gating_ref[:, here] * dot(z, norm(triangle).astype(BF16))
        return (current_ref[:, here].astype(F32) + update).astype(BF16)

    def place_of(a, a_lo):
        t = a // (n_a // 2)
        rest = a % (n_a // 2)
        return t * (n_b * LANES) + (rest // 2) * LANES + (rest % 2) * SUB + a_lo

    def place_at(c):
        return (c % 2) * 8 + (c // 2) * 2

    def pairs_of(group, i):
        for u in range(2):
            inside = i * 4 + u * 2
            number = group * (FULL // 2) + i * 2 + u
            yield inside, number // (n_a // 2), (number % (n_a // 2)) * 2

    def triangle(outgoing, inward, outward):
        def enter(group):
            inward.end(group)
            pl.when(group < WHOLE)(
                lambda: take(inward.buffers[STAGES], flat_two, group, False)
            )
            pl.when(group == WHOLE)(
                lambda: take(inward.buffers[STAGES], flat_two, group, True)
            )
            for operand in range(2):
                scatter = outgoing and operand == 1

                def some(i, operand=operand, scatter=scatter):
                    for inside, b, a in pairs_of(group, i):
                        for parity in range(2):
                            column = parity * n_b + b
                            parts = []
                            for c in range(8):
                                pieces = [
                                    flat_two[
                                        pl.ds(
                                            (place_at(c) + parity) * 2 * FULL
                                            + operand * FULL + inside + odd,
                                            n_row,
                                            stride=n_col * 2 * FULL,
                                        ),
                                        :,
                                    ]
                                    for odd in range(2)
                                ]
                                parts.append(jnp.concatenate(pieces, axis=0).astype(BF16))
                            parts = exchange(parts)
                            for a_lo in range(8):
                                if scatter:
                                    wide = parts[a_lo].astype(F32)
                                    for odd in range(2):
                                        start = place_of(a + odd, a_lo)
                                        sums[column, pl.ds(start, n_row, stride=RUN), :] = (
                                            wide[odd * n_row : (odd + 1) * n_row]
                                        )
                                else:
                                    start = pl.multiple_of(a_lo * tile + a * n_row, 16)
                                    mats[operand, column, pl.ds(start, 16), :] = parts[a_lo]

                lax.fori_loop(0, 2 - group // WHOLE, lambda i, _: (some(i), 0)[1], 0)

            def settle(b):
                for column in (b, n_b + b):
                    if outgoing:
                        mats[1, column] = sums[column].astype(BF16)
                    else:
                        left_t[column] = mats[0, column].T

            for b, complete in ((0, 1), (1, 2), (2, 4)):
                pl.when(group == complete)(functools.partial(settle, b))

        loop(GROUPS, enter)

        def multiply(b):
            if outgoing:
                whole = jnp.concatenate([mats[0, n] for n in range(tiles)], axis=1)
                both = [
                    jnp.concatenate(
                        [mats[1, k, column * LANES : (column + 1) * LANES] for k in range(tiles)],
                        axis=1,
                    )
                    for column in (b, n_b + b)
                ]
                right = jnp.concatenate(both, axis=0)
                form = (((1,), (1,)), ((), ()))
            else:
                whole = jnp.concatenate([left_t[n] for n in range(tiles)], axis=0)
                right = jnp.concatenate([mats[1, b], mats[1, n_b + b]], axis=1)
                form = (((1,), (0,)), ((), ()))
            total = lax.dot_general(whole, right, form, preferred_element_type=F32)
            sums[b] = total[:, :LANES]
            sums[n_b + b] = total[:, LANES:]

        def leave(group):
            for b, needed in ((0, 0), (1, 1), (2, 3)):
                pl.when(group == needed)(functools.partial(multiply, b))

            def some(i):
                for inside, b, a in pairs_of(group, i):
                    for parity in range(2):
                        column = parity * n_b + b
                        parts = []
                        for a_lo in range(8):
                            if outgoing:
                                start = pl.multiple_of(a_lo * tile + a * n_row, 16)
                                value = sums[column, pl.ds(start, 16), :]
                            else:
                                value = jnp.concatenate(
                                    [
                                        sums[
                                            column,
                                            pl.ds(place_of(a + odd, a_lo), n_row, stride=RUN),
                                            :,
                                        ]
                                        for odd in range(2)
                                    ],
                                    axis=0,
                                )
                            parts.append(value.astype(BF16))
                        for c, part in enumerate(exchange(parts)):
                            wide = part.astype(F32)
                            for odd in range(2):
                                flat_one[
                                    pl.ds(
                                        (place_at(c) + parity) * FULL + inside + odd,
                                        n_row,
                                        stride=n_col * FULL,
                                    ),
                                    :,
                                ] = wide[odd * n_row : (odd + 1) * n_row]

            lax.fori_loop(0, 2 - group // WHOLE, lambda i, _: (some(i), 0)[1], 0)
            pl.when(group < WHOLE)(lambda: put(flat_one, outward.buffers[0], group, False))
            pl.when(group == WHOLE)(lambda: put(flat_one, outward.buffers[0], group, True))
            outward.begin(group)

        loop(GROUPS, leave)

    ab, gate = turned(ab1_ref), turned(gate1_ref)

    def first(group, count):
        block = [x_ref[a, b, :].reshape(half * LANES, channels) for a, b in blocks_of(group, count)]
        current = jnp.concatenate(block, axis=0).astype(F32).T
        current_ref[:, lanes_of(group, count)] = current.astype(BF16)
        emit(group, count, current, ab, gate, moves[0])
        if not isinstance(group, int):
            pl.when(group == 0)(
                lambda: pl.semaphore_wait(barrier, sum(SIZES) - len(SIZES))
            )
        moves[0].begin(group)

    each_group(first)
    moves[0].advance()
    triangle(True, moves[0], moves[1])

    z, ab2, gate2 = turned(z1_ref), turned(ab2_ref), turned(gate2_ref)
    moves[1].advance()

    def middle(group, count):
        moves[1].end(group)
        current = finish(group, count, z, moves[1])
        current_ref[:, lanes_of(group, count)] = current
        emit(group, count, current.astype(F32), ab2, gate2, moves[2])
        moves[2].begin(group)

    each_group(middle)
    moves[2].advance()
    triangle(False, moves[2], moves[3])

    z2, up, down = turned(z2_ref), turned(up_ref), turned(down_ref)
    moves[3].advance()

    def last(group, count):
        moves[3].end(group)
        current = finish(group, count, z2, moves[3]).astype(F32)
        expanded = jnp.maximum(dot(up, norm(current).astype(BF16)), 0.0).astype(BF16)
        result = (current + dot(down, expanded)).T.astype(out_ref.dtype)
        for i, (a, b) in enumerate(blocks_of(group, count)):
            part = result[i * half * LANES : (i + 1) * half * LANES]
            out_ref[a, b, :] = part.reshape(half * SUB, RUN, channels)

    each_group(last)
    for move in moves:
        move.sent()


def body(
    pair,
    residue_mask,
    out_ab_weight,
    out_gate_weight,
    out_z_weight,
    in_ab_weight,
    in_gate_weight,
    in_z_weight,
    trans_up,
    trans_down,
):
    rows, cols, channels = pair.shape
    n_a, n_b = rows // SUB, cols // RUN
    chunks = n_a * n_b
    size = 8 * rows
    present = residue_mask.astype(F32)
    mask_rows = lax.dynamic_slice_in_dim(present, lax.axis_index("row") * rows, rows)
    mask_cols = lax.dynamic_slice_in_dim(present, lax.axis_index("col") * cols, cols)
    mask = (
        mask_rows.reshape(1, n_a, SUB, 1) * mask_cols.reshape(n_b, 1, 1, RUN)
    ).reshape(chunks, LANES)
    vmem = pl.BlockSpec(memory_space=pltpu.VMEM)
    buffers = []
    for rows_each in (2 * FULL, FULL, 2 * FULL, FULL):
        for _ in range(STAGES + 1):
            buffers.append(pltpu.VMEM((WHOLE,) + SIZES + (rows_each, LANES), BF16))
            buffers.append(pltpu.VMEM((1,) + SIZES + (rows_each // 2, LANES), BF16))
    return pl.pallas_call(
        kernel,
        out_shape=jax.ShapeDtypeStruct(pair.shape, pair.dtype),
        in_specs=[vmem] * 10,
        out_specs=vmem,
        scratch_shapes=[
            pltpu.VMEM((channels, chunks * LANES), BF16),
            pltpu.VMEM((channels, chunks * LANES), F32),
            pltpu.VMEM((channels * 2 * FULL, LANES), F32),
            pltpu.VMEM((channels * FULL, LANES), F32),
            pltpu.VMEM((2, size // LANES, size, LANES), BF16),
            pltpu.VMEM((size // LANES, LANES, size), BF16),
            pltpu.VMEM((size // LANES, size, LANES), F32),
            *buffers,
            pltpu.SemaphoreType.DMA((4, GROUPS, STAGES)),
            pltpu.SemaphoreType.DMA((4, GROUPS, STAGES)),
            pltpu.SemaphoreType.DMA((4, GROUPS, STAGES)),
        ],
        compiler_params=pltpu.CompilerParams(
            collective_id=0, has_side_effects=True, vmem_limit_bytes=60 << 20
        ),
    )(
        pair, mask, out_ab_weight, out_gate_weight, out_z_weight, in_ab_weight, in_gate_weight,
        in_z_weight, trans_up, trans_down,
    )


def solution(mesh):
    placed = (P("row", "col", None), P(), P(), P(), P(), P(), P(), P(), P(), P())
    return jax.shard_map(
        body, mesh=mesh, in_specs=placed, out_specs=P("row", "col", None), check_vma=False
    )
```

```python
import functools

import jax
import jax.numpy as jnp
from jax import lax
from jax.experimental import pallas as pl
from jax.experimental.pallas import tpu as pltpu
from jax.sharding import PartitionSpec as P

EPS = 1e-05
LANES = 128
SUB = 8
RUN = 16
BF16 = jnp.bfloat16
F32 = jnp.float32

SIZES = (16, 8)
STAGES = 2
FULL = 8
WHOLE = 4
GROUPS = 5
MESH = pl.DeviceIdType.MESH


def norm(x):
    center = x - jnp.mean(x, axis=0, keepdims=True)
    return center * lax.rsqrt(jnp.mean(center * center, axis=0, keepdims=True) + EPS)


def sigmoid(x):
    return 0.5 * jnp.tanh(0.5 * x) + 0.5


def dot(a, b):
    return jnp.dot(a, b, preferred_element_type=F32)


def turned(w_ref):
    return w_ref[...].astype(F32).T.astype(BF16)


def exchange(parts):
    group = lax.broadcasted_iota(jnp.int32, parts[0].shape, 1) // RUN
    parts = list(parts)
    for bit in (1, 2, 4):
        chosen = (group // bit) % 2 == 1
        for i in range(8):
            if i & bit:
                continue
            low, high = parts[i], parts[i + bit]
            parts[i] = jnp.where(chosen, pltpu.roll(high, RUN * bit, 1), low)
            parts[i + bit] = jnp.where(chosen, high, pltpu.roll(low, LANES - RUN * bit, 1))
    return parts


def coordinates():
    row, col = lax.axis_index("row"), lax.axis_index("col")
    return row * 2 + (col // 2) % 2, (col // 4) * 2 + col % 2


def device(place):
    plane, x = place
    return plane // 2, (x // 2) * 4 + (plane % 2) * 2 + x % 2


def loop(n, f, unroll=1):
    def step(i, _):
        f(i)
        return 0

    lax.fori_loop(0, n, step, 0, unroll=unroll)


def along(ref, axis, at):
    return ref.at[(slice(None),) * axis + (at,)]


class Move:
    def __init__(self, me, buffers, index, send, receive, local):
        self.me, self.buffers, self.index = me, buffers, index
        self.send, self.receive, self.local = send, receive, local

    def parts(self, group, stage):
        axis = (stage + group + self.index) % 2
        source, target = [
            whole.at[group] if group < WHOLE else last.at[0]
            for whole, last in self.buffers[stage : stage + 2]
        ]
        return axis, source, target, (self.index, group, stage)

    def start(self, group, stage):
        axis, source, target, at = self.parts(group, stage)
        here = self.me[axis]
        for step in reversed(range(1, SIZES[axis])):
            there = (here + step) % SIZES[axis]
            place = list(self.me)
            place[axis] = there
            pltpu.make_async_remote_copy(
                src_ref=along(source, axis, there),
                dst_ref=along(target, axis, here),
                send_sem=self.send.at[at],
                recv_sem=self.receive.at[at],
                device_id=device(place),
                device_id_type=MESH,
            ).start()
        pltpu.make_async_copy(
            along(source, axis, here), along(target, axis, here), self.local.at[at]
        ).start()

    def arrive(self, group, stage):
        axis, source, target, at = self.parts(group, stage)
        most = along(target, axis, slice(1, SIZES[axis]))
        pltpu.make_async_copy(most, most, self.receive.at[at]).wait()
        one = along(target, axis, self.me[axis])
        pltpu.make_async_copy(one, one, self.local.at[at]).wait()

    def sent(self):
        for group in range(GROUPS):
            for stage in range(STAGES):
                axis, source, target, at = self.parts(group, stage)
                most = along(source, axis, slice(1, SIZES[axis]))
                pltpu.make_async_copy(most, most, self.send.at[at]).wait()

    def advance(self):
        for group in range(GROUPS):
            self.arrive(group, 0)
            self.start(group, 1)

    def at_group(self, group, act):
        if isinstance(group, int):
            act(group)
            return
        for one in range(GROUPS):
            pl.when(group == one)(functools.partial(act, one))

    def begin(self, group):
        self.at_group(group, lambda one: self.start(one, 0))

    def end(self, group):
        self.at_group(group, lambda one: self.arrive(one, 1))


def spans(rows):
    return [(n * FULL, n * FULL + FULL // 2) for n in range(rows // FULL)]


def put(flat, buffers, group, short):
    whole, last = buffers
    planes, places, rows = whole.shape[1:4]

    def one(plane):
        block = flat[pl.ds(pl.multiple_of(plane * places * rows, 8), places * rows), :]
        for x in range(places):
            part = block[x * rows : (x + 1) * rows]
            if short:
                part = jnp.concatenate([part[i:j] for i, j in spans(rows)], axis=0)
                last[0, plane, x] = part.astype(BF16)
            else:
                whole[group, plane, x] = part.astype(BF16)

    loop(planes, one, 2)


def take(buffers, flat, group, short):
    whole, last = buffers
    planes, places, rows = whole.shape[1:4]

    def one(plane):
        first = pl.multiple_of(plane * places * rows, 8)
        if short:
            for x in range(places):
                part = last[0, plane, x].astype(F32)
                for n, (i, j) in enumerate(spans(rows)):
                    flat[pl.ds(first + (x * rows + i), j - i), :] = part[n * (j - i) : (n + 1) * (j - i)]
        else:
            block = [whole[group, plane, x].astype(F32) for x in range(places)]
            flat[pl.ds(first, places * rows), :] = jnp.concatenate(block, axis=0)

    loop(planes, one, 2)


def kernel(
    x_ref, mask_ref, ab1_ref, gate1_ref, z1_ref, ab2_ref, gate2_ref, z2_ref, up_ref, down_ref,
    out_ref,
    current_ref, gating_ref, flat_two, flat_one, mats, left_t, sums, mask_rows, mask_cols, *rest,
):
    n_row, n_col = 8, 16
    rows, cols, channels = x_ref.shape
    n_a, n_b = rows // SUB, cols // RUN
    tile = n_row * n_a
    tiles = 2 * n_b
    half = FULL // 2
    me = coordinates()
    buffers, (send, receive, local) = rest[:-3], rest[-3:]
    moves = []
    for index in range(4):
        mine = buffers[index * 6 : index * 6 + 6]
        pairs = [mine[i : i + 2] for i in range(0, 6, 2)]
        moves.append(Move(me, pairs, index, send, receive, local))

    barrier = pltpu.get_barrier_semaphore()
    for axis in range(len(SIZES)):
        for step in range(1, SIZES[axis]):
            place = list(me)
            place[axis] = (me[axis] + step) % SIZES[axis]
            pl.semaphore_signal(barrier, inc=1, device_id=device(place), device_id_type=MESH)

    def each_group(f):
        loop(WHOLE, lambda group: f(group, FULL))
        f(WHOLE, half)

    present = mask_ref[...].reshape(1, n_row * rows).astype(F32)
    size = present.shape[1]
    lane = lax.broadcasted_iota(jnp.int32, (size, LANES), 1)
    residue = lax.broadcasted_iota(jnp.int32, (size, LANES), 0)
    for target, begin, step, chosen in (
        (mask_rows, lax.axis_index("row") * rows, SUB, lane // RUN),
        (mask_cols, lax.axis_index("col") * cols, RUN, lane % RUN),
    ):
        line = lax.broadcasted_iota(jnp.int32, (target.shape[0], size), 0)
        index = lax.broadcasted_iota(jnp.int32, (target.shape[0], size), 1)
        mine = jnp.where(index // step - begin // step == line, present, 0.0).astype(BF16)
        target[...] = dot(mine, jnp.where(residue % step == chosen, 1.0, 0.0).astype(BF16))

    def mask_of(group, count):
        found = []
        for j in range(count):
            chunk = group * FULL + j
            found.append(
                mask_rows[pl.ds(chunk % n_a, 1), :] * mask_cols[pl.ds(chunk // n_a, 1), :]
            )
        return jnp.concatenate(found, axis=1)

    def lanes_of(group, count):
        return pl.ds(pl.multiple_of(group * (FULL * LANES), LANES), count * LANES)

    def blocks_of(group, count):
        found = []
        for i in range(count // half):
            number = group * 2 + i
            b, a = number // (n_a // half), number % (n_a // half)
            found.append(
                (
                    pl.ds(pl.multiple_of(a * (half * SUB), half * SUB), half * SUB),
                    pl.ds(pl.multiple_of(b * RUN, RUN), RUN),
                )
            )
        return found

    def emit(group, count, current, ab, gate, move):
        normed = norm(current).astype(BF16)
        hidden = ab.shape[0] // 4
        mask = mask_of(group, count)
        p = dot(ab, normed)
        left = mask * sigmoid(p[hidden : 2 * hidden]) * p[:hidden]
        right = mask * sigmoid(p[3 * hidden :]) * p[2 * hidden : 3 * hidden]
        for j in range(count):
            lanes = slice(j * LANES, (j + 1) * LANES)
            flat_two[pl.ds(j, hidden, stride=2 * FULL), :] = left[:, lanes]
            flat_two[pl.ds(FULL + j, hidden, stride=2 * FULL), :] = right[:, lanes]
        gating_ref[:, lanes_of(group, count)] = sigmoid(dot(gate, normed))
        put(flat_two, move.buffers[0], group, count < FULL)

    def finish(group, count, z, move):
        take(move.buffers[STAGES], flat_one, group, count < FULL)
        triangle = jnp.concatenate(
            [flat_one[pl.ds(j, channels, stride=FULL), :] for j in range(count)], axis=1
        )
        here = lanes_of(group, count)
        update = gating_ref[:, here] * dot(z, norm(triangle).astype(BF16))
        return (current_ref[:, here].astype(F32) + update).astype(BF16)

    def place_of(a, a_lo):
        t = a // (n_a // 2)
        rest = a % (n_a // 2)
        return t * (n_b * LANES) + (rest // 2) * LANES + (rest % 2) * SUB + a_lo

    def place_at(c):
        return (c % 2) * 8 + (c // 2) * 2

    def pairs_of(group, i):
        for u in range(2):
            inside = i * 4 + u * 2
            number = group * (FULL // 2) + i * 2 + u
            yield inside, number // (n_a // 2), (number % (n_a // 2)) * 2

    def triangle(outgoing, inward, outward):
        def enter(group):
            inward.end(group)
            pl.when(group < WHOLE)(
                lambda: take(inward.buffers[STAGES], flat_two, group, False)
            )
            pl.when(group == WHOLE)(
                lambda: take(inward.buffers[STAGES], flat_two, group, True)
            )
            for operand in range(2):
                scatter = outgoing and operand == 1

                def some(i, operand=operand, scatter=scatter):
                    for inside, b, a in pairs_of(group, i):
                        for parity in range(2):
                            column = parity * n_b + b
                            parts = []
                            for c in range(8):
                                pieces = [
                                    flat_two[
                                        pl.ds(
                                            (place_at(c) + parity) * 2 * FULL
                                            + operand * FULL + inside + odd,
                                            n_row,
                                            stride=n_col * 2 * FULL,
                                        ),
                                        :,
                                    ]
                                    for odd in range(2)
                                ]
                                parts.append(jnp.concatenate(pieces, axis=0).astype(BF16))
                            parts = exchange(parts)
                            for a_lo in range(8):
                                if scatter:
                                    wide = parts[a_lo].astype(F32)
                                    for odd in range(2):
                                        start = place_of(a + odd, a_lo)
                                        sums[column, pl.ds(start, n_row, stride=RUN), :] = (
                                            wide[odd * n_row : (odd + 1) * n_row]
                                        )
                                else:
                                    start = pl.multiple_of(a_lo * tile + a * n_row, 16)
                                    mats[operand, column, pl.ds(start, 16), :] = parts[a_lo]

                lax.fori_loop(0, 2 - group // WHOLE, lambda i, _: (some(i), 0)[1], 0)

            def settle(b):
                for column in (b, n_b + b):
                    if outgoing:
                        mats[1, column] = sums[column].astype(BF16)
                    else:
                        left_t[column] = mats[0, column].T

            for b, complete in ((0, 1), (1, 2), (2, 4)):
                pl.when(group == complete)(functools.partial(settle, b))

        loop(GROUPS, enter)

        def multiply(b):
            if outgoing:
                whole = jnp.concatenate([mats[0, n] for n in range(tiles)], axis=1)
                both = [
                    jnp.concatenate(
                        [mats[1, k, column * LANES : (column + 1) * LANES] for k in range(tiles)],
                        axis=1,
                    )
                    for column in (b, n_b + b)
                ]
                right = jnp.concatenate(both, axis=0)
                form = (((1,), (1,)), ((), ()))
            else:
                whole = jnp.concatenate([left_t[n] for n in range(tiles)], axis=0)
                right = jnp.concatenate([mats[1, b], mats[1, n_b + b]], axis=1)
                form = (((1,), (0,)), ((), ()))
            total = lax.dot_general(whole, right, form, preferred_element_type=F32)
            sums[b] = total[:, :LANES]
            sums[n_b + b] = total[:, LANES:]

        def leave(group):
            for b, needed in ((0, 0), (1, 1), (2, 3)):
                pl.when(group == needed)(functools.partial(multiply, b))

            def some(i):
                for inside, b, a in pairs_of(group, i):
                    for parity in range(2):
                        column = parity * n_b + b
                        parts = []
                        for a_lo in range(8):
                            if outgoing:
                                start = pl.multiple_of(a_lo * tile + a * n_row, 16)
                                value = sums[column, pl.ds(start, 16), :]
                            else:
                                value = jnp.concatenate(
                                    [
                                        sums[
                                            column,
                                            pl.ds(place_of(a + odd, a_lo), n_row, stride=RUN),
                                            :,
                                        ]
                                        for odd in range(2)
                                    ],
                                    axis=0,
                                )
                            parts.append(value.astype(BF16))
                        for c, part in enumerate(exchange(parts)):
                            wide = part.astype(F32)
                            for odd in range(2):
                                flat_one[
                                    pl.ds(
                                        (place_at(c) + parity) * FULL + inside + odd,
                                        n_row,
                                        stride=n_col * FULL,
                                    ),
                                    :,
                                ] = wide[odd * n_row : (odd + 1) * n_row]

            lax.fori_loop(0, 2 - group // WHOLE, lambda i, _: (some(i), 0)[1], 0)
            pl.when(group < WHOLE)(lambda: put(flat_one, outward.buffers[0], group, False))
            pl.when(group == WHOLE)(lambda: put(flat_one, outward.buffers[0], group, True))
            outward.begin(group)

        loop(GROUPS, leave)

    ab, gate = turned(ab1_ref), turned(gate1_ref)

    def first(group, count):
        block = [x_ref[a, b, :].reshape(half * LANES, channels) for a, b in blocks_of(group, count)]
        current = jnp.concatenate(block, axis=0).astype(F32).T
        current_ref[:, lanes_of(group, count)] = current.astype(BF16)
        emit(group, count, current, ab, gate, moves[0])
        if not isinstance(group, int):
            pl.when(group == 0)(
                lambda: pl.semaphore_wait(barrier, sum(SIZES) - len(SIZES))
            )
        moves[0].begin(group)

    each_group(first)
    moves[0].advance()
    triangle(True, moves[0], moves[1])

    z, ab2, gate2 = turned(z1_ref), turned(ab2_ref), turned(gate2_ref)
    moves[1].advance()

    def middle(group, count):
        moves[1].end(group)
        current = finish(group, count, z, moves[1])
        current_ref[:, lanes_of(group, count)] = current
        emit(group, count, current.astype(F32), ab2, gate2, moves[2])
        moves[2].begin(group)

    each_group(middle)
    moves[2].advance()
    triangle(False, moves[2], moves[3])

    z2, up, down = turned(z2_ref), turned(up_ref), turned(down_ref)
    moves[3].advance()

    def last(group, count):
        moves[3].end(group)
        current = finish(group, count, z2, moves[3]).astype(F32)
        expanded = jnp.maximum(dot(up, norm(current).astype(BF16)), 0.0).astype(BF16)
        result = (current + dot(down, expanded)).T.astype(out_ref.dtype)
        for i, (a, b) in enumerate(blocks_of(group, count)):
            part = result[i * half * LANES : (i + 1) * half * LANES]
            out_ref[a, b, :] = part.reshape(half * SUB, RUN, channels)

    each_group(last)
    for move in moves:
        move.sent()


def body(
    pair,
    residue_mask,
    out_ab_weight,
    out_gate_weight,
    out_z_weight,
    in_ab_weight,
    in_gate_weight,
    in_z_weight,
    trans_up,
    trans_down,
):
    rows, cols, channels = pair.shape
    n_a, n_b = rows // SUB, cols // RUN
    chunks = n_a * n_b
    size = 8 * rows
    vmem = pl.BlockSpec(memory_space=pltpu.VMEM)
    buffers = []
    for rows_each in (2 * FULL, FULL, 2 * FULL, FULL):
        for _ in range(STAGES + 1):
            buffers.append(pltpu.VMEM((WHOLE,) + SIZES + (rows_each, LANES), BF16))
            buffers.append(pltpu.VMEM((1,) + SIZES + (rows_each // 2, LANES), BF16))
    return pl.pallas_call(
        kernel,
        out_shape=jax.ShapeDtypeStruct(pair.shape, pair.dtype),
        in_specs=[vmem] * 10,
        out_specs=vmem,
        scratch_shapes=[
            pltpu.VMEM((channels, chunks * LANES), BF16),
            pltpu.VMEM((channels, chunks * LANES), F32),
            pltpu.VMEM((channels * 2 * FULL, LANES), F32),
            pltpu.VMEM((channels * FULL, LANES), F32),
            pltpu.VMEM((2, size // LANES, size, LANES), BF16),
            pltpu.VMEM((size // LANES, LANES, size), BF16),
            pltpu.VMEM((size // LANES, size, LANES), F32),
            pltpu.VMEM((16, LANES), F32),
            pltpu.VMEM((8, LANES), F32),
            *buffers,
            pltpu.SemaphoreType.DMA((4, GROUPS, STAGES)),
            pltpu.SemaphoreType.DMA((4, GROUPS, STAGES)),
            pltpu.SemaphoreType.DMA((4, GROUPS, STAGES)),
        ],
        compiler_params=pltpu.CompilerParams(
            collective_id=0, has_side_effects=True, vmem_limit_bytes=60 << 20
        ),
    )(
        pair, residue_mask, out_ab_weight, out_gate_weight, out_z_weight, in_ab_weight, in_gate_weight,
        in_z_weight, trans_up, trans_down,
    )


def solution(mesh):
    placed = (P("row", "col", None), P(), P(), P(), P(), P(), P(), P(), P(), P())
    return jax.shard_map(
        body, mesh=mesh, in_specs=placed, out_specs=P("row", "col", None), check_vma=False
    )
```

```python
import functools

import jax
import jax.numpy as jnp
from jax import lax
from jax.experimental import pallas as pl
from jax.experimental.pallas import tpu as pltpu
from jax.sharding import PartitionSpec as P

EPS = 1e-05
LANES = 128
SUB = 8
RUN = 16
BF16 = jnp.bfloat16
F32 = jnp.float32

SIZES = (16, 8)
STAGES = 2
FULL = 8
WHOLE = 4
GROUPS = 5
MESH = pl.DeviceIdType.MESH


def norm(x):
    center = x - jnp.mean(x, axis=0, keepdims=True)
    return center * lax.rsqrt(jnp.mean(center * center, axis=0, keepdims=True) + EPS)


def sigmoid(x):
    return 0.5 * jnp.tanh(0.5 * x) + 0.5


def dot(a, b):
    return jnp.dot(a, b, preferred_element_type=F32)


def turned(w_ref):
    return w_ref[...].astype(F32).T.astype(BF16)


def exchange(parts):
    group = lax.broadcasted_iota(jnp.int32, parts[0].shape, 1) // RUN
    parts = list(parts)
    for bit in (1, 2, 4):
        chosen = (group // bit) % 2 == 1
        for i in range(8):
            if i & bit:
                continue
            low, high = parts[i], parts[i + bit]
            parts[i] = jnp.where(chosen, pltpu.roll(high, RUN * bit, 1), low)
            parts[i + bit] = jnp.where(chosen, high, pltpu.roll(low, LANES - RUN * bit, 1))
    return parts


def coordinates():
    row, col = lax.axis_index("row"), lax.axis_index("col")
    return row * 2 + (col // 2) % 2, (col // 4) * 2 + col % 2


def device(place):
    plane, x = place
    return plane // 2, (x // 2) * 4 + (plane % 2) * 2 + x % 2


def loop(n, f, unroll=1):
    def step(i, _):
        f(i)
        return 0

    lax.fori_loop(0, n, step, 0, unroll=unroll)


def along(ref, axis, at):
    return ref.at[(slice(None),) * axis + (at,)]


class Move:
    def __init__(self, me, buffers, index, send, receive, local):
        self.me, self.buffers, self.index = me, buffers, index
        self.send, self.receive, self.local = send, receive, local

    def parts(self, group, stage):
        axis = (stage + group + self.index) % 2
        source, target = [
            whole.at[group] if group < WHOLE else last.at[0]
            for whole, last in self.buffers[stage : stage + 2]
        ]
        return axis, source, target, (self.index, group, stage)

    def start(self, group, stage):
        axis, source, target, at = self.parts(group, stage)
        here = self.me[axis]
        for step in reversed(range(1, SIZES[axis])):
            there = (here + step) % SIZES[axis]
            place = list(self.me)
            place[axis] = there
            pltpu.make_async_remote_copy(
                src_ref=along(source, axis, there),
                dst_ref=along(target, axis, here),
                send_sem=self.send.at[at],
                recv_sem=self.receive.at[at],
                device_id=device(place),
                device_id_type=MESH,
            ).start()
        pltpu.make_async_copy(
            along(source, axis, here), along(target, axis, here), self.local.at[at]
        ).start()

    def arrive(self, group, stage):
        axis, source, target, at = self.parts(group, stage)
        most = along(target, axis, slice(1, SIZES[axis]))
        pltpu.make_async_copy(most, most, self.receive.at[at]).wait()
        one = along(target, axis, self.me[axis])
        pltpu.make_async_copy(one, one, self.local.at[at]).wait()

    def sent(self):
        for group in range(GROUPS):
            for stage in range(STAGES):
                axis, source, target, at = self.parts(group, stage)
                most = along(source, axis, slice(1, SIZES[axis]))
                pltpu.make_async_copy(most, most, self.send.at[at]).wait()

    def advance(self):
        for group in range(GROUPS):
            self.arrive(group, 0)
            self.start(group, 1)

    def at_group(self, group, act):
        if isinstance(group, int):
            act(group)
            return
        for one in range(GROUPS):
            pl.when(group == one)(functools.partial(act, one))

    def begin(self, group):
        self.at_group(group, lambda one: self.start(one, 0))

    def end(self, group):
        self.at_group(group, lambda one: self.arrive(one, 1))


def spans(rows):
    return [(n * FULL, n * FULL + FULL // 2) for n in range(rows // FULL)]


def put(flat, buffers, group, short):
    whole, last = buffers
    planes, places, rows = whole.shape[1:4]

    def one(plane):
        block = flat[pl.ds(pl.multiple_of(plane * places * rows, 8), places * rows), :]
        for x in range(places):
            part = block[x * rows : (x + 1) * rows]
            if short:
                part = jnp.concatenate([part[i:j] for i, j in spans(rows)], axis=0)
                last[0, plane, x] = part.astype(BF16)
            else:
                whole[group, plane, x] = part.astype(BF16)

    loop(planes, one, 4)


def take(buffers, flat, group, short):
    whole, last = buffers
    planes, places, rows = whole.shape[1:4]

    def one(plane):
        first = pl.multiple_of(plane * places * rows, 8)
        if short:
            for x in range(places):
                part = last[0, plane, x].astype(F32)
                for n, (i, j) in enumerate(spans(rows)):
                    flat[pl.ds(first + (x * rows + i), j - i), :] = part[n * (j - i) : (n + 1) * (j - i)]
        else:
            block = [whole[group, plane, x].astype(F32) for x in range(places)]
            flat[pl.ds(first, places * rows), :] = jnp.concatenate(block, axis=0)

    loop(planes, one, 4)


def kernel(
    x_ref, mask_ref, ab1_ref, gate1_ref, z1_ref, ab2_ref, gate2_ref, z2_ref, up_ref, down_ref,
    out_ref,
    current_ref, gating_ref, flat_two, flat_one, mats, left_t, sums, mask_rows, mask_cols, *rest,
):
    n_row, n_col = 8, 16
    rows, cols, channels = x_ref.shape
    n_a, n_b = rows // SUB, cols // RUN
    tile = n_row * n_a
    tiles = 2 * n_b
    half = FULL // 2
    me = coordinates()
    buffers, (send, receive, local) = rest[:-3], rest[-3:]
    moves = []
    for index in range(4):
        mine = buffers[index * 6 : index * 6 + 6]
        pairs = [mine[i : i + 2] for i in range(0, 6, 2)]
        moves.append(Move(me, pairs, index, send, receive, local))

    barrier = pltpu.get_barrier_semaphore()
    for axis in range(len(SIZES)):
        for step in range(1, SIZES[axis]):
            place = list(me)
            place[axis] = (me[axis] + step) % SIZES[axis]
            pl.semaphore_signal(barrier, inc=1, device_id=device(place), device_id_type=MESH)

    def each_group(f):
        loop(WHOLE, lambda group: f(group, FULL))
        f(WHOLE, half)

    present = mask_ref[...].reshape(1, n_row * rows).astype(F32)
    size = present.shape[1]
    lane = lax.broadcasted_iota(jnp.int32, (size, LANES), 1)
    residue = lax.broadcasted_iota(jnp.int32, (size, LANES), 0)
    for target, begin, step, chosen in (
        (mask_rows, lax.axis_index("row") * rows, SUB, lane // RUN),
        (mask_cols, lax.axis_index("col") * cols, RUN, lane % RUN),
    ):
        line = lax.broadcasted_iota(jnp.int32, (target.shape[0], size), 0)
        index = lax.broadcasted_iota(jnp.int32, (target.shape[0], size), 1)
        mine = jnp.where(index // step - begin // step == line, present, 0.0).astype(BF16)
        target[...] = dot(mine, jnp.where(residue % step == chosen, 1.0, 0.0).astype(BF16))

    def mask_of(group, count):
        found = []
        for j in range(count):
            chunk = group * FULL + j
            found.append(
                mask_rows[pl.ds(chunk % n_a, 1), :] * mask_cols[pl.ds(chunk // n_a, 1), :]
            )
        return jnp.concatenate(found, axis=1)

    def lanes_of(group, count):
        return pl.ds(pl.multiple_of(group * (FULL * LANES), LANES), count * LANES)

    def blocks_of(group, count):
        found = []
        for i in range(count // half):
            number = group * 2 + i
            b, a = number // (n_a // half), number % (n_a // half)
            found.append(
                (
                    pl.ds(pl.multiple_of(a * (half * SUB), half * SUB), half * SUB),
                    pl.ds(pl.multiple_of(b * RUN, RUN), RUN),
                )
            )
        return found

    def emit(group, count, current, ab, gate, move):
        normed = norm(current).astype(BF16)
        hidden = ab.shape[0] // 4
        mask = mask_of(group, count)
        p = dot(ab, normed)
        left = mask * sigmoid(p[hidden : 2 * hidden]) * p[:hidden]
        right = mask * sigmoid(p[3 * hidden :]) * p[2 * hidden : 3 * hidden]
        for j in range(count):
            lanes = slice(j * LANES, (j + 1) * LANES)
            flat_two[pl.ds(j, hidden, stride=2 * FULL), :] = left[:, lanes]
            flat_two[pl.ds(FULL + j, hidden, stride=2 * FULL), :] = right[:, lanes]
        gating_ref[:, lanes_of(group, count)] = sigmoid(dot(gate, normed))
        put(flat_two, move.buffers[0], group, count < FULL)

    def finish(group, count, z, move):
        take(move.buffers[STAGES], flat_one, group, count < FULL)
        triangle = jnp.concatenate(
            [flat_one[pl.ds(j, channels, stride=FULL), :] for j in range(count)], axis=1
        )
        here = lanes_of(group, count)
        update = gating_ref[:, here] * dot(z, norm(triangle).astype(BF16))
        return (current_ref[:, here].astype(F32) + update).astype(BF16)

    def place_of(a, a_lo):
        t = a // (n_a // 2)
        rest = a % (n_a // 2)
        return t * (n_b * LANES) + (rest // 2) * LANES + (rest % 2) * SUB + a_lo

    def place_at(c):
        return (c % 2) * 8 + (c // 2) * 2

    def pairs_of(group, i):
        for u in range(2):
            inside = i * 4 + u * 2
            number = group * (FULL // 2) + i * 2 + u
            yield inside, number // (n_a // 2), (number % (n_a // 2)) * 2

    def triangle(outgoing, inward, outward):
        def enter(group):
            inward.end(group)
            pl.when(group < WHOLE)(
                lambda: take(inward.buffers[STAGES], flat_two, group, False)
            )
            pl.when(group == WHOLE)(
                lambda: take(inward.buffers[STAGES], flat_two, group, True)
            )
            for operand in range(2):
                scatter = outgoing and operand == 1

                def some(i, operand=operand, scatter=scatter):
                    for inside, b, a in pairs_of(group, i):
                        for parity in range(2):
                            column = parity * n_b + b
                            parts = []
                            for c in range(8):
                                pieces = [
                                    flat_two[
                                        pl.ds(
                                            (place_at(c) + parity) * 2 * FULL
                                            + operand * FULL + inside + odd,
                                            n_row,
                                            stride=n_col * 2 * FULL,
                                        ),
                                        :,
                                    ]
                                    for odd in range(2)
                                ]
                                parts.append(jnp.concatenate(pieces, axis=0).astype(BF16))
                            parts = exchange(parts)
                            for a_lo in range(8):
                                if scatter:
                                    wide = parts[a_lo].astype(F32)
                                    for odd in range(2):
                                        start = place_of(a + odd, a_lo)
                                        sums[column, pl.ds(start, n_row, stride=RUN), :] = (
                                            wide[odd * n_row : (odd + 1) * n_row]
                                        )
                                else:
                                    start = pl.multiple_of(a_lo * tile + a * n_row, 16)
                                    mats[operand, column, pl.ds(start, 16), :] = parts[a_lo]

                lax.fori_loop(0, 2 - group // WHOLE, lambda i, _: (some(i), 0)[1], 0)

            def settle(b):
                for column in (b, n_b + b):
                    if outgoing:
                        mats[1, column] = sums[column].astype(BF16)
                    else:
                        left_t[column] = mats[0, column].T

            for b, complete in ((0, 1), (1, 2), (2, 4)):
                pl.when(group == complete)(functools.partial(settle, b))

        loop(GROUPS, enter)

        def multiply(b):
            if outgoing:
                whole = jnp.concatenate([mats[0, n] for n in range(tiles)], axis=1)
                both = [
                    jnp.concatenate(
                        [mats[1, k, column * LANES : (column + 1) * LANES] for k in range(tiles)],
                        axis=1,
                    )
                    for column in (b, n_b + b)
                ]
                right = jnp.concatenate(both, axis=0)
                form = (((1,), (1,)), ((), ()))
            else:
                whole = jnp.concatenate([left_t[n] for n in range(tiles)], axis=0)
                right = jnp.concatenate([mats[1, b], mats[1, n_b + b]], axis=1)
                form = (((1,), (0,)), ((), ()))
            total = lax.dot_general(whole, right, form, preferred_element_type=F32)
            sums[b] = total[:, :LANES]
            sums[n_b + b] = total[:, LANES:]

        def leave(group):
            for b, needed in ((0, 0), (1, 1), (2, 3)):
                pl.when(group == needed)(functools.partial(multiply, b))

            def some(i):
                for inside, b, a in pairs_of(group, i):
                    for parity in range(2):
                        column = parity * n_b + b
                        parts = []
                        for a_lo in range(8):
                            if outgoing:
                                start = pl.multiple_of(a_lo * tile + a * n_row, 16)
                                value = sums[column, pl.ds(start, 16), :]
                            else:
                                value = jnp.concatenate(
                                    [
                                        sums[
                                            column,
                                            pl.ds(place_of(a + odd, a_lo), n_row, stride=RUN),
                                            :,
                                        ]
                                        for odd in range(2)
                                    ],
                                    axis=0,
                                )
                            parts.append(value.astype(BF16))
                        for c, part in enumerate(exchange(parts)):
                            wide = part.astype(F32)
                            for odd in range(2):
                                flat_one[
                                    pl.ds(
                                        (place_at(c) + parity) * FULL + inside + odd,
                                        n_row,
                                        stride=n_col * FULL,
                                    ),
                                    :,
                                ] = wide[odd * n_row : (odd + 1) * n_row]

            lax.fori_loop(0, 2 - group // WHOLE, lambda i, _: (some(i), 0)[1], 0)
            pl.when(group < WHOLE)(lambda: put(flat_one, outward.buffers[0], group, False))
            pl.when(group == WHOLE)(lambda: put(flat_one, outward.buffers[0], group, True))
            outward.begin(group)

        loop(GROUPS, leave)

    ab, gate = turned(ab1_ref), turned(gate1_ref)

    def first(group, count):
        block = [x_ref[a, b, :].reshape(half * LANES, channels) for a, b in blocks_of(group, count)]
        current = jnp.concatenate(block, axis=0).astype(F32).T
        current_ref[:, lanes_of(group, count)] = current.astype(BF16)
        emit(group, count, current, ab, gate, moves[0])
        if not isinstance(group, int):
            pl.when(group == 0)(
                lambda: pl.semaphore_wait(barrier, sum(SIZES) - len(SIZES))
            )
        moves[0].begin(group)

    each_group(first)
    moves[0].advance()
    triangle(True, moves[0], moves[1])

    z, ab2, gate2 = turned(z1_ref), turned(ab2_ref), turned(gate2_ref)
    moves[1].advance()

    def middle(group, count):
        moves[1].end(group)
        current = finish(group, count, z, moves[1])
        current_ref[:, lanes_of(group, count)] = current
        emit(group, count, current.astype(F32), ab2, gate2, moves[2])
        moves[2].begin(group)

    each_group(middle)
    moves[2].advance()
    triangle(False, moves[2], moves[3])

    z2, up, down = turned(z2_ref), turned(up_ref), turned(down_ref)
    for move in moves[:3]:
        move.sent()
    moves[3].advance()

    def last(group, count):
        moves[3].end(group)
        current = finish(group, count, z2, moves[3]).astype(F32)
        expanded = jnp.maximum(dot(up, norm(current).astype(BF16)), 0.0).astype(BF16)
        result = (current + dot(down, expanded)).T.astype(out_ref.dtype)
        for i, (a, b) in enumerate(blocks_of(group, count)):
            part = result[i * half * LANES : (i + 1) * half * LANES]
            out_ref[a, b, :] = part.reshape(half * SUB, RUN, channels)

    each_group(last)
    moves[3].sent()


def body(
    pair,
    residue_mask,
    out_ab_weight,
    out_gate_weight,
    out_z_weight,
    in_ab_weight,
    in_gate_weight,
    in_z_weight,
    trans_up,
    trans_down,
):
    rows, cols, channels = pair.shape
    n_a, n_b = rows // SUB, cols // RUN
    chunks = n_a * n_b
    size = 8 * rows
    vmem = pl.BlockSpec(memory_space=pltpu.VMEM)
    buffers = []
    for rows_each in (2 * FULL, FULL, 2 * FULL, FULL):
        for _ in range(STAGES + 1):
            buffers.append(pltpu.VMEM((WHOLE,) + SIZES + (rows_each, LANES), BF16))
            buffers.append(pltpu.VMEM((1,) + SIZES + (rows_each // 2, LANES), BF16))
    return pl.pallas_call(
        kernel,
        out_shape=jax.ShapeDtypeStruct(pair.shape, pair.dtype),
        in_specs=[vmem] * 10,
        out_specs=vmem,
        scratch_shapes=[
            pltpu.VMEM((channels, chunks * LANES), BF16),
            pltpu.VMEM((channels, chunks * LANES), F32),
            pltpu.VMEM((channels * 2 * FULL, LANES), F32),
            pltpu.VMEM((channels * FULL, LANES), F32),
            pltpu.VMEM((2, size // LANES, size, LANES), BF16),
            pltpu.VMEM((size // LANES, LANES, size), BF16),
            pltpu.VMEM((size // LANES, size, LANES), F32),
            pltpu.VMEM((16, LANES), F32),
            pltpu.VMEM((8, LANES), F32),
            *buffers,
            pltpu.SemaphoreType.DMA((4, GROUPS, STAGES)),
            pltpu.SemaphoreType.DMA((4, GROUPS, STAGES)),
            pltpu.SemaphoreType.DMA((4, GROUPS, STAGES)),
        ],
        compiler_params=pltpu.CompilerParams(
            collective_id=0, has_side_effects=True, vmem_limit_bytes=60 << 20
        ),
    )(
        pair, residue_mask, out_ab_weight, out_gate_weight, out_z_weight, in_ab_weight, in_gate_weight,
        in_z_weight, trans_up, trans_down,
    )


def solution(mesh):
    placed = (P("row", "col", None), P(), P(), P(), P(), P(), P(), P(), P(), P())
    return jax.shard_map(
        body, mesh=mesh, in_specs=placed, out_specs=P("row", "col", None), check_vma=False
    )
```
